32 devices in a mesh: brick: 32 (over z, y, x, core).
Axes of the slice: x: 2, y: 2, z: 4, core: 2. Of those that a mesh axis runs over, the one named last changes fastest.
Arguments:
- sensitivity: float32 [32, 65536], P(None, 'brick'), may hold values from -40 to 40
- diagonal: float32 [65536], P('brick'), may hold values from 1 to 16
- displacement: bfloat16 [65536], P('brick'), may hold values from -3 to 3
- connectivity: int32 [4096, 128], P('brick'), may hold values from 0 to 2559
- normal_stiff: float32 [4096], P('brick'), may hold values from 0.5 to 2
- shear_stiff: float32 [4096], P('brick'), may hold values from 0.3 to 1.5
- friction: float32 [4096], P('brick'), may hold values from 0.3 to 0.8
- slip_state: int32 [4096], P('brick'), may hold values 0 or 1
- owner_map: int32 [32, 2, 256], P('brick'), may hold values from 0 to 255, each once within a row
- templates: bfloat16 [3, 128, 128], replicated, may hold values from -0.25 to 0.25
Outputs:
- adjoint: float32 [32, 65536], P(None, 'brick')
- joint_grads: float32 [3, 32, 4096], P(None, None, 'brick')
The draws below stay inside these ranges and needn't reach their ends.
Inputs may be any that keep to these rules, and one draw needn't show every extreme that they name: connectivity[e, i] names a slot of the extended field of element e's brick. For each brick and side, owner_map is a permutation of 0 .. 255.
All inputs are finite; a program needn't handle non-finite values. No bound on the sum of `slip_state` on one device may be relied on, other than what follows from the above.
Results may differ from the reference program's by a relative error of at most 0.0042.
The reference program's roundings to bfloat16 on the way (of `extended`, `scaled`, `adjoint_half` and `pushed`) count: a program that leaves them out, or rounds other values in their place, can miss the bound.
Values may be sent and summed in bfloat16 or wider, within the bound.
No kernel may reach another device: no remote copies, remote signals or barrier semaphores. Data moves between devices by JAX's collectives and lax.ppermute only.
A program may use at most 64 MiB of HBM per device.

```python
import math
import jax
import jax.numpy as jnp
from jax import lax

NOBJ = 32
ELEM_DOF = 128
ITERS = 2
DOF_DEV = 2048
ELEM_DEV = 128
GHOST = 256
EXT = 2560
DOFS = 65536
ELEMS = 4096
N_BRICK = 32


def brick_positions(key):
    return jax.random.uniform(jax.random.fold_in(key, 7), (N_BRICK,), jnp.float32, 0.0, 1.0)


def draw_diagonal(key, part):
    level = jnp.exp(brick_positions(key) * math.log(8.0))
    key_factor = jax.random.fold_in(key, 11)
    factor = jnp.exp(jax.random.uniform(key_factor, (DOFS,), jnp.float32, 0.0, math.log(2.0)))
    return jnp.clip(jnp.repeat(level, DOF_DEV) * factor, 1.0, 16.0)


def draw_sensitivity(key, part):
    position_brick = brick_positions(key)
    key_row, key_col, key_mix, key_shared, key_own = jax.random.split(jax.random.fold_in(key, 13), 5)
    centers = (jnp.arange(8, dtype=jnp.float32) + 0.5) / 8.0
    profile = jnp.exp(-jnp.square((position_brick[None, :] - centers[:, None]) / 0.09))
    profile = jnp.repeat(profile, DOF_DEV, axis=1)
    mixing = jax.random.normal(key_mix, (NOBJ, 8), jnp.float32)
    row_scale = jnp.exp(jax.random.uniform(key_row, (NOBJ, 1), jnp.float32, 0.0, math.log(10.0)))
    col_scale = jnp.exp(jax.random.uniform(key_col, (1, DOFS), jnp.float32, 0.0, math.log(10.0)))
    position = jnp.arange(DOFS, dtype=jnp.float32)[None, :] / DOFS
    growth = jnp.exp(position * 0.5 * math.log(3.0))
    shared = jax.random.normal(key_shared, (8, DOFS), jnp.float32)
    own_part = jax.random.normal(key_own, (NOBJ, DOFS), jnp.float32)
    mixed = 0.5 * own_part
    for member in range(8):
        mixed = mixed + mixing[:, member:member + 1] * (profile[member] * shared[member])[None, :]
    mixed = jnp.clip(mixed, -4.0, 4.0)
    return jnp.clip(0.1 * row_scale * col_scale * growth * mixed, -40.0, 40.0)


def plant(values, stream_key, least, high):
    longest = values.shape.index(max(values.shape))
    spots = []
    for shift in (0, 1):
        where = [jax.random.randint(jax.random.fold_in(stream_key, axis), (), 0, length) for axis, length in enumerate(values.shape)]
        where[longest] = (where[longest] + shift) % values.shape[longest]
        spots.append(tuple(where))
    return values.at[spots[0]].set(least).at[spots[1]].set(high)


def block_levels(own_key, shape, cuts, low, high):
    loudness = 1.0
    for dim, parts in cuts:
        draws = jax.random.uniform(jax.random.fold_in(jax.random.fold_in(own_key, 6), dim), (parts,), jnp.float32, low / len(cuts), high / len(cuts))
        loudness = loudness * jnp.repeat(jnp.exp(draws), shape[dim] // parts).reshape((-1,) + (1,) * (len(shape) - 1 - dim))
    return loudness


def bell_draw(stream_key, shape, deviation, limit, shards=(), kind=jnp.bfloat16):
    factor_of = block_levels(stream_key, shape, shards, -0.22, 0.18) if shards else 1.0
    array = jax.random.normal(stream_key, shape, jnp.float32) * deviation * factor_of
    return jnp.minimum(jnp.maximum(array, -limit), limit).astype(kind)


def setup_inputs(seed: int = 0) -> dict:
    streams_of = jax.random.split(jax.random.key(seed), 11)
    return {
        "sensitivity": draw_sensitivity(jax.random.fold_in(streams_of[10], 71), 0),
        "diagonal": draw_diagonal(jax.random.fold_in(streams_of[10], 71), 0),
        "displacement": bell_draw(streams_of[2], (DOFS,), 0.5, 3.0, ((0, 32),)),
        "connectivity": plant(jax.random.randint(streams_of[3], (ELEMS, ELEM_DOF), 0, EXT), jax.random.fold_in(streams_of[3], 1), 0, EXT - 1).astype(jnp.int32),
        "normal_stiff": jnp.clip(jnp.exp(math.log(2.0) - 1.3862944 * jax.random.uniform(streams_of[4], (ELEMS,), jnp.float32) ** block_levels(streams_of[4], (ELEMS,), ((0, 32),), -0.2, 0.2)), 0.5, 2.0),
        "shear_stiff": jnp.clip(jnp.exp(math.log(1.5) - 1.60943787 * jax.random.uniform(streams_of[5], (ELEMS,), jnp.float32) ** block_levels(streams_of[5], (ELEMS,), ((0, 32),), -0.2, 0.2)), 0.3, 1.5),
        "friction": jnp.clip(0.3 + 0.5 * jax.random.uniform(streams_of[6], (ELEMS,), jnp.float32) ** block_levels(streams_of[6], (ELEMS,), ((0, 32),), -0.2, 0.2), 0.3, 0.8),
        "slip_state": plant((jax.random.randint(streams_of[7], (ELEMS,), 0, 2) < 1).astype(jnp.int32), jax.random.fold_in(streams_of[7], 1), 0, 1),
        "owner_map": jax.vmap(lambda own: jax.random.permutation(own, GHOST))(jax.random.split(streams_of[8], N_BRICK * 2)).reshape((N_BRICK, 2, GHOST)).astype(jnp.int32),
        "templates": bell_draw(streams_of[9], (3, ELEM_DOF, ELEM_DOF), (4 * ELEM_DOF) ** -0.5, 0.25),
    }


FULL_PRECISION = lax.Precision.HIGHEST

def inner(first, second):
    return jnp.dot(first.astype(jnp.float32), second.T.astype(jnp.float32), precision=FULL_PRECISION, preferred_element_type=jnp.float32)

def lower_inverse(gram_matrix):
    factor = jnp.linalg.cholesky(gram_matrix)
    identity = jnp.eye(gram_matrix.shape[0], dtype=jnp.float32)
    return (jax.scipy.linalg.solve_triangular(factor, identity, lower=True), factor)

def element_partials(extended, connectivity, stiff_coeffs, templates):
    rows = extended.shape[0]
    width = extended.shape[1]
    elem_count = connectivity.shape[0]
    block_size = min(elem_count, 64)
    blocks = elem_count // block_size
    slot_count = templates.shape[1]
    stacked = templates.reshape(3 * slot_count, slot_count)
    connect_blocks = connectivity.reshape(blocks, block_size, slot_count)
    coeff_blocks = stiff_coeffs.reshape(3, blocks, block_size).transpose(1, 0, 2)

    def one_block(total, inputs):
        block_conn, block_coeff = inputs
        values = extended[:, block_conn]
        scaled = (values[:, :, None, :].astype(jnp.float32) * block_coeff.T[None, :, :, None]).astype(jnp.bfloat16)
        result = jnp.dot(scaled.reshape(rows * block_size, 3 * slot_count).astype(jnp.float32), stacked.astype(jnp.float32), preferred_element_type=jnp.float32)
        total = total.at[:, block_conn].add(result.reshape(rows, block_size, slot_count))
        return (total, None)
    total, unused = lax.scan(one_block, jnp.zeros((rows, width), jnp.float32), (connect_blocks, coeff_blocks))
    return total

def bands(whole):
    rows = whole.shape[0]
    per_brick = whole.reshape(rows, N_BRICK, DOF_DEV).transpose(1, 0, 2)
    empty = jnp.zeros((1, rows, GHOST), whole.dtype)
    lower_band = jnp.concatenate([empty, per_brick[:-1, :, DOF_DEV - GHOST:]], axis=0)
    upper_band = jnp.concatenate([per_brick[1:, :, :GHOST], empty], axis=0)
    return (per_brick, lower_band, upper_band)

def extend(own_rows, lower_band, upper_band, owner_pair):
    return jnp.concatenate([lower_band[:, owner_pair[0]], own_rows, upper_band[:, owner_pair[1]]], axis=1)

def apply_operator(half, current, diagonal, connectivity, stiff_coeffs, owner_map, templates):
    rows = half.shape[0]
    per_brick, lower_band, upper_band = bands(half)
    connect_bricks = connectivity.reshape(N_BRICK, ELEM_DEV, ELEM_DOF)
    coeff_bricks = stiff_coeffs.reshape(3, N_BRICK, ELEM_DEV).transpose(1, 0, 2)

    def one_brick(inputs):
        own_rows, brick_lower, brick_upper, brick_conn, brick_coeff, owner_pair = inputs
        partial_value = element_partials(extend(own_rows, brick_lower, brick_upper, owner_pair), brick_conn, brick_coeff, templates)
        empty = jnp.zeros((rows, GHOST), jnp.float32)
        to_lower = empty.at[:, owner_pair[0]].add(partial_value[:, :GHOST])
        to_upper = empty.at[:, owner_pair[1]].add(partial_value[:, GHOST + DOF_DEV:])
        return (partial_value[:, GHOST:GHOST + DOF_DEV], to_lower, to_upper)
    owned, to_lower, to_upper = lax.map(one_brick, (per_brick, lower_band, upper_band, connect_bricks, coeff_bricks, owner_map))
    empty = jnp.zeros((1, rows, GHOST), jnp.float32)
    from_upper = jnp.concatenate([to_lower[1:], empty], axis=0)
    from_lower = jnp.concatenate([empty, to_upper[:-1]], axis=0)
    owned = owned.at[:, :, DOF_DEV - GHOST:].add(from_upper)
    owned = owned.at[:, :, :GHOST].add(from_lower)
    return diagonal[None, :] * current + owned.transpose(1, 0, 2).reshape(rows, DOFS)

def project_out(image, projections, basis):
    reduced = image
    for earlier in range(projections.shape[0]):
        reduced = reduced - jnp.dot(projections[earlier].T.astype(jnp.float32), basis[earlier].astype(jnp.float32), precision=FULL_PRECISION, preferred_element_type=jnp.float32)
    return reduced

def least_squares(projections, factors):
    count = factors[0].shape[0]
    iterations = len(projections)
    hessenberg = jnp.zeros(((iterations + 1) * count, iterations * count), jnp.float32)
    for column in range(iterations):
        for block_row in range(column + 1):
            hessenberg = hessenberg.at[block_row * count:(block_row + 1) * count, column * count:(column + 1) * count].set(projections[column][block_row])
        hessenberg = hessenberg.at[(column + 1) * count:(column + 2) * count, column * count:(column + 1) * count].set(factors[column + 1].T)
    target = jnp.zeros(((iterations + 1) * count, count), jnp.float32).at[:count].set(factors[0].T)
    normal_matrix = jnp.dot(hessenberg.T.astype(jnp.float32), hessenberg.astype(jnp.float32), precision=FULL_PRECISION, preferred_element_type=jnp.float32)
    right_side = jnp.dot(hessenberg.T.astype(jnp.float32), target.astype(jnp.float32), precision=FULL_PRECISION, preferred_element_type=jnp.float32)
    cholesky_factor = jnp.linalg.cholesky(normal_matrix)
    return jax.scipy.linalg.cho_solve((cholesky_factor, True), right_side)

def combine(weights, fields):
    count = weights.shape[1]
    total = jnp.dot(weights[:count].T.astype(jnp.float32), fields[0].astype(jnp.float32), precision=FULL_PRECISION, preferred_element_type=jnp.float32)
    for column in range(1, len(fields)):
        total = total + jnp.dot(weights[column * count:(column + 1) * count].T.astype(jnp.float32), fields[column].astype(jnp.float32), precision=FULL_PRECISION, preferred_element_type=jnp.float32)
    return total

def element_gradients(adjoint_ext, displace_ext, connectivity, normal_stiff, friction, slip_real, templates):
    displace_elem = displace_ext[connectivity].astype(jnp.float32)
    pushed = jnp.einsum('ej,kij->eki', displace_elem, templates.astype(jnp.float32), precision=FULL_PRECISION).astype(jnp.bfloat16)
    adjoint_elem = adjoint_ext[:, connectivity].astype(jnp.float32)
    pairs = jnp.einsum('oei,eki->koe', adjoint_elem, pushed.astype(jnp.float32), precision=FULL_PRECISION)
    grad_normal = -(pairs[0] + (slip_real * friction)[None, :] * pairs[2])
    grad_shear = -pairs[1]
    grad_friction = -(slip_real * normal_stiff)[None, :] * pairs[2]
    return jnp.stack([grad_normal, grad_shear, grad_friction])

def reference(sensitivity, diagonal, displacement, connectivity, normal_stiff, shear_stiff, friction, slip_state, owner_map, templates):
    slip_real = slip_state.astype(jnp.float32)
    stiff_coeffs = jnp.stack([normal_stiff, shear_stiff, slip_real * friction * normal_stiff])
    inverse, factor = lower_inverse(inner(sensitivity, sensitivity))
    basis = [jnp.dot(inverse.astype(jnp.float32), sensitivity.astype(jnp.float32), precision=FULL_PRECISION, preferred_element_type=jnp.float32)]
    halves = []
    projections = []
    factors = [factor]
    for column in range(ITERS):
        half = basis[column].astype(jnp.bfloat16)
        halves.append(half)
        image = apply_operator(half, basis[column], diagonal, connectivity, stiff_coeffs, owner_map, templates)
        current_proj = jnp.stack([inner(basis[earlier], image) for earlier in range(column + 1)])
        reduced = project_out(image, current_proj, basis)
        inverse, factor = lower_inverse(inner(reduced, reduced))
        projections.append(current_proj)
        factors.append(factor)
        if column + 1 < ITERS:
            basis.append(jnp.dot(inverse.astype(jnp.float32), reduced.astype(jnp.float32), precision=FULL_PRECISION, preferred_element_type=jnp.float32))
    weights = least_squares(projections, factors)
    adjoint = combine(weights, basis)
    adjoint_half = combine(weights, halves).astype(jnp.bfloat16)
    adjoint_own, adjoint_lower, adjoint_upper = bands(adjoint_half)
    displace_own, displace_lower, displace_upper = bands(displacement[None, :])

    def brick_grads(inputs):
        adj_rows, adj_lower, adj_upper, disp_rows, disp_lower, disp_upper, brick_conn, owner_pair, brick_normal, brick_friction, brick_slip = inputs
        adjoint_ext = extend(adj_rows, adj_lower, adj_upper, owner_pair)
        displace_ext = extend(disp_rows, disp_lower, disp_upper, owner_pair)[0]
        return element_gradients(adjoint_ext, displace_ext, brick_conn, brick_normal, brick_friction, brick_slip, templates)
    grads = lax.map(brick_grads, (adjoint_own, adjoint_lower, adjoint_upper, displace_own, displace_lower, displace_upper, connectivity.reshape(N_BRICK, ELEM_DEV, ELEM_DOF), owner_map, normal_stiff.reshape(N_BRICK, ELEM_DEV), friction.reshape(N_BRICK, ELEM_DEV), slip_real.reshape(N_BRICK, ELEM_DEV)))
    joint_grads = grads.transpose(1, 2, 0, 3).reshape(3, NOBJ, ELEMS)
    return (adjoint, joint_grads)
```

```python
import functools

import jax
import jax.numpy as jnp
from jax import lax
from jax.experimental import pallas as pl
from jax.experimental.pallas import tpu as pltpu
from jax.sharding import PartitionSpec as P

LO = 256
CHUNK = 8
VMEM_LIMIT = 40 * 1024 * 1024
F32 = jnp.float32
BF16 = jnp.bfloat16
NN = (((1,), (0,)), ((), ()))
NT = (((1,), (1,)), ((), ()))
TN = (((0,), (0,)), ((), ()))


def fdot(a, b, dims=NN):
    return lax.dot_general(a, b, dims, precision=lax.Precision.HIGHEST, preferred_element_type=F32)


def bdot(a, b, dims=NN):
    return lax.dot_general(a, b, dims, preferred_element_type=F32)


def eye(n):
    return (
        lax.broadcasted_iota(jnp.int32, (n, n), 0) == lax.broadcasted_iota(jnp.int32, (n, n), 1)
    ).astype(F32)


def lower_inverse(gram):
    n = gram.shape[0]
    row_id = lax.broadcasted_iota(jnp.int32, (n, n), 0)
    col_id = lax.broadcasted_iota(jnp.int32, (n, n), 1)
    work, side = gram, eye(n)
    for k in range(n):
        pivot = work[k : k + 1, k : k + 1]
        step = jnp.where(row_id[:, :1] > k, work[:, k : k + 1] / pivot, 0.0)
        side = side - step * side[k : k + 1, :]
        work = work - step * work[k : k + 1, :]
    diag = jnp.sum(jnp.where(row_id == col_id, work, 0.0), axis=1, keepdims=True)
    scale = 1.0 / jnp.sqrt(diag)
    return side * scale, jnp.where(col_id >= row_id, work, 0.0) * scale


def one_hot(lo_rows):
    lane = lax.broadcasted_iota(jnp.int32, (LO, lo_rows.shape[1]), 0)
    return jnp.concatenate(
        [
            jnp.where(lane == lo_rows[e : e + 1, :], 1.0, 0.0).astype(BF16)
            for e in range(lo_rows.shape[0])
        ],
        axis=1,
    )


def stack_tiles(field):
    return jnp.concatenate(
        [field[:, h * LO : (h + 1) * LO] for h in range(field.shape[1] // LO)], axis=0
    )


def gathered(tiles, hot, hi_rows, rows):
    spread = bdot(tiles, hot)
    slots = hi_rows.shape[1]
    values = []
    for e in range(hi_rows.shape[0]):
        value = jnp.zeros((rows, slots), F32)
        for h in range(tiles.shape[0] // rows):
            value = jnp.where(
                hi_rows[e : e + 1, :] == h,
                spread[h * rows : (h + 1) * rows, e * slots : (e + 1) * slots],
                value,
            )
        values.append(value)
    return values


def apply_elements(half, hi_ref, lo_ref, coeff_ref, stacked_ref, tiles_ref, total_ref):
    rows, width = half.shape
    tiles = width // LO
    elems, slots = lo_ref.shape
    tiles_ref[...] = stack_tiles(half)
    total_ref[...] = jnp.zeros_like(total_ref)

    def chunk(step, carry):
        start = pl.multiple_of(step * CHUNK, CHUNK)
        hi_rows = hi_ref[pl.ds(start, CHUNK), :]
        hot = one_hot(lo_ref[pl.ds(start, CHUNK), :])
        values = gathered(tiles_ref[...], hot, hi_rows, rows)
        scaled = jnp.concatenate(
            [
                jnp.concatenate(
                    [(values[e] * coeff_ref[k, start + e]).astype(BF16) for k in range(3)], axis=1
                )
                for e in range(CHUNK)
            ],
            axis=0,
        )
        result = bdot(scaled, stacked_ref[...])
        spread = jnp.concatenate(
            [
                jnp.concatenate(
                    [
                        jnp.where(
                            hi_rows[e : e + 1, :] == h, result[e * rows : (e + 1) * rows, :], 0.0
                        ).astype(BF16)
                        for e in range(CHUNK)
                    ],
                    axis=1,
                )
                for h in range(tiles)
            ],
            axis=0,
        )
        total_ref[...] += bdot(spread, hot, NT)
        return carry

    lax.fori_loop(0, elems // CHUNK, chunk, 0)
    return jnp.concatenate([total_ref[h * rows : (h + 1) * rows, :] for h in range(tiles)], axis=1)


def write_image(basis, partial, diag_ref, image_ref, low_ref, high_ref, ghost):
    width = basis.shape[1]
    own = diag_ref[...] * basis[:, ghost : width - ghost] + partial[:, ghost : width - ghost]
    owned = own.shape[1]
    image_ref[:, :ghost] = partial[:, :ghost]
    image_ref[:, ghost : width - ghost] = own
    image_ref[:, width - ghost :] = partial[:, width - ghost :]
    low_ref[:, :ghost] = own[:, :ghost]
    low_ref[:, ghost:] = partial[:, :ghost]
    high_ref[:, :ghost] = own[:, owned - ghost :]
    high_ref[:, ghost:] = partial[:, width - ghost :]


def prepare_kernel(edge_ref, conn_ref, owner_ref, disp_ref, templ_ref, hi_ref, lo_ref, push_ref, elem_ref):
    elems, slots = conn_ref.shape
    last = disp_ref.shape[0] - 1
    first_hi = edge_ref[0]
    last_hi = edge_ref[1]
    owner = owner_ref[...].astype(F32).astype(BF16)
    disp = disp_ref[...]

    def chunk(step, carry):
        start = pl.multiple_of(step * CHUNK, CHUNK)
        conn = conn_ref[pl.ds(start, CHUNK), :]
        hi = conn // LO
        lo = conn - hi * LO
        renamed = bdot(owner, one_hot(lo))
        below = jnp.concatenate(
            [renamed[0:1, e * slots : (e + 1) * slots] for e in range(CHUNK)], axis=0
        ).astype(jnp.int32)
        above = jnp.concatenate(
            [renamed[1:2, e * slots : (e + 1) * slots] for e in range(CHUNK)], axis=0
        ).astype(jnp.int32)
        lo = jnp.where(hi == 0, below, jnp.where(hi == last, above, lo))
        hi = jnp.where((hi < first_hi) | (hi > last_hi), -1, hi)
        hi_ref[pl.ds(start, CHUNK), :] = hi
        lo_ref[pl.ds(start, CHUNK), :] = lo
        spread = bdot(disp, one_hot(lo))
        hi_id = lax.broadcasted_iota(jnp.int32, (last + 1, slots), 0)
        elem_ref[pl.ds(start, CHUNK), :] = jnp.concatenate(
            [
                jnp.sum(
                    jnp.where(
                        hi_id == hi[e : e + 1, :], spread[:, e * slots : (e + 1) * slots], 0.0
                    ),
                    axis=0,
                    keepdims=True,
                )
                for e in range(CHUNK)
            ],
            axis=0,
        )
        return carry

    lax.fori_loop(0, elems // CHUNK, chunk, 0)
    values = elem_ref[...].astype(BF16)
    for k in range(3):
        push_ref[:, k * elems : (k + 1) * elems] = bdot(templ_ref[k], values, NT).astype(BF16)


def first_kernel(
    gram_ref, sens_ref, low_in, high_in, diag_ref, hi_ref, lo_ref, coeff_ref, stacked_ref,
    basis_ref, image_ref, low_ref, high_ref, factor_ref, tiles_ref, total_ref,
):
    ghost = low_in.shape[1]
    inverse, factor = lower_inverse(gram_ref[...])
    factor_ref[...] = factor
    basis = jnp.concatenate(
        [fdot(inverse, low_in[...]), fdot(inverse, sens_ref[...]), fdot(inverse, high_in[...])], axis=1
    )
    basis_ref[...] = basis
    partial = apply_elements(
        basis.astype(BF16), hi_ref, lo_ref, coeff_ref, stacked_ref, tiles_ref, total_ref
    )
    write_image(basis, partial, diag_ref, image_ref, low_ref, high_ref, ghost)


def complete(image_ref, low_in, high_in, full_ref):
    width = image_ref.shape[1]
    ghost = low_in.shape[1] // 2
    full_ref[:, :ghost] = image_ref[:, :ghost] + low_in[:, :ghost]
    full_ref[:, ghost : 2 * ghost] = image_ref[:, ghost : 2 * ghost] + low_in[:, ghost:]
    full_ref[:, 2 * ghost : width - 2 * ghost] = image_ref[:, 2 * ghost : width - 2 * ghost]
    full_ref[:, width - 2 * ghost : width - ghost] = (
        image_ref[:, width - 2 * ghost : width - ghost] + high_in[:, ghost:]
    )
    full_ref[:, width - ghost :] = image_ref[:, width - ghost :] + high_in[:, :ghost]


def gram_kernel(*refs):
    *basis_refs, image_ref, low_in, high_in, full_ref, gram_ref = refs
    complete(image_ref, low_in, high_in, full_ref)
    ghost = low_in.shape[1] // 2
    width = full_ref.shape[1]
    own = full_ref[:, ghost : width - ghost]
    for place, ref in enumerate(basis_refs):
        gram_ref[place] = fdot(ref[:, ghost : width - ghost], own, NT)
    gram_ref[len(basis_refs)] = fdot(own, own, NT)


def second_kernel(
    gram_ref, basis0_ref, full_ref, diag_ref, hi_ref, lo_ref, coeff_ref, stacked_ref,
    basis_ref, image_ref, low_ref, high_ref, factor_ref, tiles_ref, total_ref,
):
    ghost = low_ref.shape[1] // 2
    proj = gram_ref[0]
    inverse, factor = lower_inverse(gram_ref[1] - fdot(proj, proj, TN))
    factor_ref[...] = factor
    reduced = full_ref[...] - fdot(proj, basis0_ref[...], TN)
    basis = fdot(inverse, reduced)
    basis_ref[...] = basis
    partial = apply_elements(
        basis.astype(BF16), hi_ref, lo_ref, coeff_ref, stacked_ref, tiles_ref, total_ref
    )
    write_image(basis, partial, diag_ref, image_ref, low_ref, high_ref, ghost)


def last_kernel(
    gram0_ref, gram1_ref, factor0_ref, factor1_ref, basis0_ref, basis1_ref, hi_ref, lo_ref, push_ref,
    sticks_ref, adjoint_ref, grads_ref, tiles_ref, pairs_ref,
):
    rows, width = basis0_ref.shape
    ghost = (width - adjoint_ref.shape[1]) // 2
    elems, slots = lo_ref.shape
    p00, n00 = gram0_ref[0], gram0_ref[1]
    p01, p11, n11 = gram1_ref[0], gram1_ref[1], gram1_ref[2]
    upper0, upper1 = factor0_ref[...], factor1_ref[...]
    head, unused = lower_inverse(n00)
    head_side = fdot(head, fdot(p00, upper0, TN))
    n01 = fdot(p00, p01, TN) + fdot(upper1, p11, TN)
    cross = fdot(head, n01)
    tail, unused = lower_inverse(n11 - fdot(cross, cross, TN))
    tail_side = fdot(tail, fdot(p01, upper0, TN) - fdot(cross, head_side, TN))
    w1 = fdot(tail, tail_side, TN)
    w0 = fdot(head, head_side - fdot(cross, w1), TN)
    basis0, basis1 = basis0_ref[...], basis1_ref[...]
    adjoint_ref[...] = fdot(w0, basis0[:, ghost : width - ghost], TN) + fdot(
        w1, basis1[:, ghost : width - ghost], TN
    )
    half0, half1 = basis0.astype(BF16).astype(F32), basis1.astype(BF16).astype(F32)
    tiles_ref[...] = stack_tiles((fdot(w0, half0, TN) + fdot(w1, half1, TN)).astype(BF16))
    pairs_ref[...] = jnp.zeros_like(pairs_ref)
    lane = lax.broadcasted_iota(jnp.int32, (rows, 3 * elems), 1) % elems

    def chunk(step, carry):
        start = pl.multiple_of(step * CHUNK, CHUNK)
        hot = one_hot(lo_ref[pl.ds(start, CHUNK), :])
        values = gathered(tiles_ref[...], hot, hi_ref[pl.ds(start, CHUNK), :], rows)
        every = bdot(jnp.concatenate(values, axis=0).astype(BF16), push_ref[...])
        pairs = pairs_ref[...]
        for e in range(CHUNK):
            pairs = jnp.where(lane == start + e, every[e * rows : (e + 1) * rows, :], pairs)
        pairs_ref[...] = pairs
        return carry

    lax.fori_loop(0, elems // CHUNK, chunk, 0)
    third = pairs_ref[:, 2 * elems :]
    grads_ref[0] = -(pairs_ref[:, :elems] + sticks_ref[0:1, :] * third)
    grads_ref[1] = -pairs_ref[:, elems : 2 * elems]
    grads_ref[2] = -sticks_ref[1:2, :] * third


def call(kernel, outs, scratch, args, smem=()):
    return pl.pallas_call(
        kernel,
        out_shape=[jax.ShapeDtypeStruct(shape, dtype) for shape, dtype in outs],
        in_specs=[
            pl.BlockSpec(memory_space=pltpu.SMEM if i in smem else pltpu.VMEM)
            for i in range(len(args))
        ],
        out_specs=[pl.BlockSpec(memory_space=pltpu.VMEM) for unused in outs],
        scratch_shapes=[pltpu.VMEM(shape, dtype) for shape, dtype in scratch],
        compiler_params=pltpu.CompilerParams(vmem_limit_bytes=VMEM_LIMIT),
    )(*args)


def total(value, axis):
    count = lax.axis_size(axis)
    stride = 1
    while stride < count:
        left = count // stride
        radix = 2 if stride == 1 or left % 4 else 4
        parts = [value]
        for d in range(1, radix):
            route = []
            for i in range(count):
                digit = (i // stride) % radix
                route.append((i, i + ((digit ^ d) - digit) * stride))
            parts.append(lax.ppermute(value, axis, route))
        while len(parts) > 1:
            parts = [parts[2 * i] + parts[2 * i + 1] for i in range(len(parts) // 2)]
        value = parts[0]
        stride *= radix
    return value


def on_device(
    sensitivity, diagonal, displacement, connectivity, normal_stiff, shear_stiff, friction, slip_state,
    owner_map, templates,
):
    axis = "brick"
    count = lax.axis_size(axis)
    me = lax.axis_index(axis)
    up = [(i, i + 1) for i in range(count - 1)]
    down = [(i + 1, i) for i in range(count - 1)]
    rows, owned = sensitivity.shape
    ghost = owner_map.shape[2]
    elems, slots = connectivity.shape
    width = owned + 2 * ghost
    tiles = width // LO
    wide = ((rows, width), F32)
    band = ((rows, 2 * ghost), F32)
    small = ((rows, rows), F32)
    work = [((tiles * rows, LO), BF16), ((tiles * rows, LO), F32)]

    gram = fdot(sensitivity, sensitivity, NT)
    low_sens = lax.ppermute(sensitivity[:, owned - ghost :], axis, up)
    high_sens = lax.ppermute(sensitivity[:, :ghost], axis, down)
    low_disp = lax.ppermute(displacement[owned - ghost :], axis, up)
    high_disp = lax.ppermute(displacement[:ghost], axis, down)
    gram = total(gram, axis)

    slip = slip_state.astype(F32)
    coeffs = jnp.stack([normal_stiff, shear_stiff, slip * friction * normal_stiff])
    sticks = jnp.stack([slip * friction, slip * normal_stiff])
    stacked = templates.reshape(3 * slots, slots)
    diag_row = diagonal[None, :]
    edges = jnp.stack([jnp.where(me == 0, 1, 0), jnp.where(me == count - 1, tiles - 2, tiles - 1)])
    disp_tiles = jnp.concatenate([low_disp, displacement, high_disp]).reshape(tiles, LO)
    hi, lo, pushed = call(
        prepare_kernel,
        [((elems, slots), jnp.int32), ((elems, slots), jnp.int32), ((slots, 3 * elems), BF16)],
        [((elems, slots), F32)],
        [edges.astype(jnp.int32), connectivity, owner_map[0], disp_tiles, templates],
        smem=(0,),
    )

    basis0, image, low, high, factor0 = call(
        first_kernel,
        [wide, wide, band, band, small],
        work,
        [gram, sensitivity, low_sens, high_sens, diag_row, hi, lo, coeffs, stacked],
        smem=(7,),
    )
    low, high = lax.ppermute(high, axis, up), lax.ppermute(low, axis, down)
    full, gram0 = call(
        gram_kernel, [wide, ((2, rows, rows), F32)], [], [basis0, image, low, high]
    )
    gram0 = total(gram0, axis)

    basis1, image, low, high, factor1 = call(
        second_kernel,
        [wide, wide, band, band, small],
        work,
        [gram0, basis0, full, diag_row, hi, lo, coeffs, stacked],
        smem=(6,),
    )
    low, high = lax.ppermute(high, axis, up), lax.ppermute(low, axis, down)
    unused, gram1 = call(
        gram_kernel, [wide, ((3, rows, rows), F32)], [], [basis0, basis1, image, low, high]
    )
    gram1 = total(gram1, axis)

    adjoint, grads = call(
        last_kernel,
        [((rows, owned), F32), ((3, rows, elems), F32)],
        [((tiles * rows, LO), BF16), ((rows, 3 * elems), F32)],
        [gram0, gram1, factor0, factor1, basis0, basis1, hi, lo, pushed, sticks],
    )
    return adjoint, grads


def solution(mesh):
    in_specs = (
        P(None, "brick"),
        P("brick"),
        P("brick"),
        P("brick", None),
        P("brick"),
        P("brick"),
        P("brick"),
        P("brick"),
        P("brick", None, None),
        P(),
    )
    out_specs = (P(None, "brick"), P(None, None, "brick"))
    return jax.shard_map(
        on_device, mesh=mesh, in_specs=in_specs, out_specs=out_specs, check_vma=False
    )
```

```python
import jax
import jax.numpy as jnp
from jax import lax
from jax.experimental import pallas as pl
from jax.experimental.pallas import tpu as pltpu
from jax.sharding import PartitionSpec as P

CHUNK = 16
PIVOTS = 4
VMEM_LIMIT = 48 * 1024 * 1024
AXIS = "brick"
F32 = jnp.float32
BF16 = jnp.bfloat16
NN = (((1,), (0,)), ((), ()))
NT = (((1,), (1,)), ((), ()))
TN = (((0,), (0,)), ((), ()))


def fdot(a, b, dims=NN):
    return lax.dot_general(a, b, dims, precision=lax.Precision.HIGHEST, preferred_element_type=F32)


def bdot(a, b, dims=NN):
    return lax.dot_general(a, b, dims, preferred_element_type=F32)


def lower_inverse(gram):
    n = gram.shape[0]
    row_id = lax.broadcasted_iota(jnp.int32, (n, n), 0)
    col_id = lax.broadcasted_iota(jnp.int32, (n, n), 1)
    work, side = gram, jnp.where(row_id == col_id, 1.0, 0.0).astype(F32)
    for first in range(0, n, PIVOTS):
        places = range(first, first + PIVOTS)
        cols = [jnp.broadcast_to(work[:, k : k + 1], (n, n)) for k in places]
        rows = [work[k : k + 1, :] for k in places]
        sides = [side[k : k + 1, :] for k in places]
        for j, k in enumerate(places):
            step = jnp.where(row_id > k, cols[j] * (1.0 / cols[j][k : k + 1, :]), 0.0)
            for m in range(j + 1, PIVOTS):
                at = first + m
                cols[m] = cols[m] - step * cols[j][at : at + 1, :]
                rows[m] = rows[m] - step[at : at + 1, :] * rows[j]
                sides[m] = sides[m] - step[at : at + 1, :] * sides[j]
            work = work - step * rows[j]
            side = side - step * sides[j]
    diag = jnp.sum(jnp.where(row_id == col_id, work, 0.0), axis=1, keepdims=True)
    scale = 1.0 / jnp.sqrt(diag)
    return side * scale, jnp.where(col_id >= row_id, work, 0.0) * scale


def packed(square):
    n = square.shape[0]
    fold = 128 // n
    part = n // fold
    return jnp.concatenate([square[j * part : (j + 1) * part, :] for j in range(fold)], axis=1)


def unpacked(tile):
    n = int((tile.shape[0] * 128) ** 0.5)
    fold = 128 // n
    return jnp.concatenate([tile[:, j * n : (j + 1) * n] for j in range(fold)], axis=0)


def tall(row, count):
    return jnp.broadcast_to(row, (count, row.shape[1])).astype(BF16)


def one_hot(lo_rows, depth):
    slots = lo_rows.shape[1]
    place = lax.broadcasted_iota(jnp.int32, (depth, slots), 0).astype(F32).astype(BF16)
    one, zero = jnp.ones((), BF16), jnp.zeros((), BF16)
    return jnp.concatenate(
        [
            jnp.where(place == tall(lo_rows[e : e + 1, :], depth), one, zero)
            for e in range(lo_rows.shape[0])
        ],
        axis=1,
    )


def apply_elements(
    half, conn_ref, owner_ref, coeff_ref, stacked_ref, values_ref, tiles_ref, total_ref,
    state=None, state_ref=None,
):
    rows, width = half.shape
    depth = owner_ref.shape[1]
    count = width // depth
    elems, slots = conn_ref.shape
    owner = owner_ref[...].astype(F32)
    below, above = one_hot(owner[0:1, :], depth), one_hot(owner[1:2, :], depth)
    tiles_ref[:rows, :] = bdot(half[:, :depth], below).astype(BF16)
    for h in range(1, count - 1):
        tiles_ref[h * rows : (h + 1) * rows, :] = half[:, h * depth : (h + 1) * depth]
    tiles_ref[(count - 1) * rows : count * rows, :] = bdot(half[:, width - depth :], above).astype(BF16)
    if state is not None:
        extra = tiles_ref.shape[0] - count * rows
        pieces = [state[:, h * depth : (h + 1) * depth] for h in range(count)]
        pieces[0] = bdot(tall(pieces[0], 16), below)[0:1, :]
        pieces[-1] = bdot(tall(pieces[-1], 16), above)[0:1, :]
        pieces.append(jnp.zeros((extra - count, depth), F32))
        tiles_ref[count * rows :, :] = jnp.concatenate(pieces, axis=0).astype(BF16)
    total_ref[...] = jnp.zeros_like(total_ref)
    zero = jnp.zeros((), BF16)

    def chunk(step, carry):
        start = pl.multiple_of(step * CHUNK, CHUNK)
        conn = conn_ref[pl.ds(start, CHUNK), :]
        hi = lax.div(conn, depth)
        hot = one_hot((conn - hi * depth).astype(F32), depth)
        spread = bdot(tiles_ref[...], hot)
        hi_wide = [tall(hi[e : e + 1, :].astype(F32), rows) for e in range(CHUNK)]
        scaled = []
        for e in range(CHUNK):
            here = slice(e * slots, (e + 1) * slots)
            value = spread[:rows, here]
            for h in range(1, count):
                value = jnp.where(
                    hi[e : e + 1, :] == h, spread[h * rows : (h + 1) * rows, here], value
                )
            values_ref[pl.ds(pl.multiple_of((start + e) * rows, rows), rows), :] = value.astype(BF16)
            scaled.append(
                jnp.concatenate(
                    [(value * coeff_ref[k, start + e]).astype(BF16) for k in range(3)], axis=1
                )
            )
            if state is not None:
                picked = spread[count * rows :, here]
                match = lax.broadcasted_iota(jnp.int32, picked.shape, 0) == hi[e : e + 1, :]
                state_ref[pl.ds(start + e, 1), :] = jnp.sum(
                    jnp.where(match, picked, 0.0), axis=0, keepdims=True
                )
        result = bdot(jnp.concatenate(scaled, axis=0), stacked_ref[...]).astype(BF16)
        masked = jnp.concatenate(
            [
                jnp.concatenate(
                    [
                        jnp.where(
                            hi_wide[e] == jnp.full((), h, BF16),
                            result[e * rows : (e + 1) * rows, :],
                            zero,
                        )
                        for e in range(CHUNK)
                    ],
                    axis=1,
                )
                for h in range(count)
            ],
            axis=0,
        )
        total_ref[...] += bdot(masked, hot, NT)
        return carry

    lax.fori_loop(0, elems // CHUNK, chunk, 0, unroll=True)
    parts = [total_ref[h * rows : (h + 1) * rows, :] for h in range(count)]
    for at, match in ((0, below), (count - 1, above)):
        top = parts[at].astype(BF16)
        rest = (parts[at] - top.astype(F32)).astype(BF16)
        both = bdot(jnp.concatenate([top, rest], axis=0), match, NT)
        parts[at] = both[:rows] + both[rows:]
    return parts


def send_bands(low, high, a_ref, b_ref):
    odd = lax.axis_index(AXIS) % 2 == 1
    a_ref[...] = jnp.where(odd, low, high)
    b_ref[...] = jnp.where(odd, high, low)


def received_bands(a_ref, b_ref):
    odd = lax.axis_index(AXIS) % 2 == 1
    a, b = a_ref[...], b_ref[...]
    return jnp.where(odd, a, b), jnp.where(odd, b, a)


def write_image(basis, parts, diag_ref, image_ref, a_ref, b_ref):
    rows, width = basis.shape
    depth = parts[0].shape[1]
    me = lax.axis_index(AXIS)
    low = parts[0] * jnp.where(me == 0, 0.0, 1.0)
    high = parts[-1] * jnp.where(me == lax.axis_size(AXIS) - 1, 0.0, 1.0)
    own = [
        diag_ref[:, (h - 1) * depth : h * depth] * basis[:, h * depth : (h + 1) * depth] + parts[h]
        for h in range(1, len(parts) - 1)
    ]
    image_ref[...] = jnp.concatenate([low] + own + [high], axis=1)
    send_bands(
        jnp.concatenate([own[0], low], axis=1), jnp.concatenate([own[-1], high], axis=1), a_ref, b_ref
    )


def complete(image_ref, a_ref, b_ref):
    depth = a_ref.shape[1] // 2
    width = image_ref.shape[1]
    low, high = received_bands(a_ref, b_ref)
    return jnp.concatenate(
        [
            image_ref[:, : 2 * depth] + low,
            image_ref[:, 2 * depth : width - 2 * depth],
            image_ref[:, width - 2 * depth :] + jnp.concatenate([high[:, depth:], high[:, :depth]], axis=1),
        ],
        axis=1,
    )


def begin_kernel(
    sens_ref, disp_ref, normal_ref, shear_ref, friction_ref, slip_ref, gram_ref, a_ref, b_ref, coeff_ref
):
    sens = sens_ref[...]
    depth = a_ref.shape[1]
    owned = sens.shape[1]
    gram = packed(fdot(sens, sens, NT))
    gram_ref[...] = jnp.broadcast_to(gram[None], gram_ref.shape)
    spare = jnp.zeros((a_ref.shape[0] - sens.shape[0] - 1, depth), F32)
    disp = disp_ref[...].astype(F32)
    low = jnp.concatenate([sens[:, :depth], disp[:, :depth], spare], axis=0)
    high = jnp.concatenate([sens[:, owned - depth :], disp[:, owned - depth :], spare], axis=0)
    send_bands(low, high, a_ref, b_ref)
    coeff_ref[0:1, :] = normal_ref[...]
    coeff_ref[1:2, :] = shear_ref[...]
    coeff_ref[2:3, :] = slip_ref[...].astype(F32) * friction_ref[...] * normal_ref[...]


def first_kernel(
    gram_ref, sens_ref, disp_ref, a_in, b_in, diag_ref, conn_ref, owner_ref, coeff_ref, stacked_ref,
    basis_ref, image_ref, a_ref, b_ref, factor_ref, values_ref, push_ref,
    tiles_ref, total_ref, state_ref,
):
    rows = sens_ref.shape[0]
    slots = conn_ref.shape[1]
    elems = conn_ref.shape[0]
    inverse, factor = lower_inverse(unpacked(jnp.sum(gram_ref[...], axis=0)))
    factor_ref[...] = factor
    low, high = received_bands(a_in, b_in)
    basis = fdot(inverse, jnp.concatenate([low[:rows], sens_ref[...], high[:rows]], axis=1))
    basis_ref[...] = basis
    state = jnp.concatenate(
        [low[rows : rows + 1], disp_ref[...].astype(F32), high[rows : rows + 1]], axis=1
    )
    parts = apply_elements(
        basis.astype(BF16), conn_ref, owner_ref, coeff_ref, stacked_ref, values_ref, tiles_ref,
        total_ref, state, state_ref,
    )
    write_image(basis, parts, diag_ref, image_ref, a_ref, b_ref)
    moved = state_ref[...].astype(BF16)
    for k in range(3):
        push_ref[:, k * elems : (k + 1) * elems] = bdot(
            stacked_ref[k * slots : (k + 1) * slots, :], moved, NT
        ).astype(BF16)


def own_part(field, depth):
    return field[:, depth : field.shape[1] - depth]


def middle_kernel(basis_ref, image_ref, a_in, b_in, full_ref, gram_ref):
    depth = a_in.shape[1] // 2
    full = complete(image_ref, a_in, b_in)
    full_ref[...] = full
    own = own_part(full, depth)
    rows = own.shape[0]
    both = fdot(jnp.concatenate([own_part(basis_ref[...], depth), own], axis=0), own, NT)
    tile = jnp.concatenate([packed(both[:rows]), packed(both[rows:])], axis=0)
    gram_ref[...] = jnp.broadcast_to(tile[None], gram_ref.shape)


def second_kernel(
    gram_ref, factor0_ref, basis0_ref, full_ref, diag_ref, conn_ref, owner_ref, coeff_ref, stacked_ref,
    basis_ref, image_ref, a_ref, b_ref, small_ref, values_ref, tiles_ref, total_ref,
):
    tile = jnp.sum(gram_ref[...], axis=0)
    part = tile.shape[0] // 2
    proj, square = unpacked(tile[:part]), unpacked(tile[part:])
    inverse, factor = lower_inverse(square - fdot(proj, proj, TN))
    head, unused = lower_inverse(square)
    reduced = full_ref[...] - fdot(proj, basis0_ref[...], TN)
    basis = fdot(inverse, reduced)
    basis_ref[...] = basis
    small_ref[0] = head
    small_ref[1] = fdot(head, proj, NT)
    small_ref[2] = fdot(head, factor, NT)
    small_ref[3] = fdot(head, fdot(proj, factor0_ref[...], TN))
    parts = apply_elements(
        basis.astype(BF16), conn_ref, owner_ref, coeff_ref, stacked_ref, values_ref, tiles_ref, total_ref
    )
    write_image(basis, parts, diag_ref, image_ref, a_ref, b_ref)


def late_kernel(basis0_ref, basis1_ref, image_ref, a_in, b_in, gram_ref):
    depth = a_in.shape[1] // 2
    own = own_part(complete(image_ref, a_in, b_in), depth)
    rows = own.shape[0]
    every = fdot(
        jnp.concatenate(
            [own_part(basis0_ref[...], depth), own_part(basis1_ref[...], depth), own], axis=0
        ),
        own,
        NT,
    )
    gram_ref[...] = jnp.concatenate(
        [packed(every[j * rows : (j + 1) * rows]) for j in range(3)], axis=0
    )


def split3(value):
    first = value.astype(BF16)
    rest = value - first.astype(F32)
    second = rest.astype(BF16)
    return jnp.concatenate([first, second, (rest - second.astype(F32)).astype(BF16)], axis=0)


def last_kernel(
    gram_ref, factor0_ref, small_ref, basis0_ref, basis1_ref, values0_ref, values1_ref, push_ref,
    normal_ref, friction_ref, slip_ref, adjoint_ref, grads_ref, pairs_ref,
):
    rows, width = basis0_ref.shape
    depth = (width - adjoint_ref.shape[1]) // 2
    elems = normal_ref.shape[1]
    slots = values0_ref.shape[1]
    part = gram_ref.shape[0] // 3
    p01, p11, n11 = (unpacked(gram_ref[j * part : (j + 1) * part, :]) for j in range(3))
    upper0 = factor0_ref[...]
    head, head_side = small_ref[0], small_ref[3]
    cross = fdot(small_ref[1], p01) + fdot(small_ref[2], p11)
    tail, unused = lower_inverse(n11 - fdot(cross, cross, TN))
    tail_side = fdot(tail, fdot(p01, upper0, TN) - fdot(cross, head_side, TN))
    w1 = fdot(tail, tail_side, TN)
    turned = jnp.concatenate(
        [fdot(head_side - fdot(cross, w1), head, TN), fdot(tail_side, tail, TN)], axis=1
    )
    adjoint_ref[...] = fdot(
        turned,
        jnp.concatenate(
            [own_part(basis0_ref[...], depth), own_part(basis1_ref[...], depth)], axis=0
        ),
    )
    weights = split3(turned)
    pairs_ref[...] = jnp.zeros_like(pairs_ref)
    lane = lax.broadcasted_iota(jnp.int32, (rows, 3 * elems), 1) % elems

    def chunk(step, carry):
        start = pl.multiple_of(step * CHUNK, CHUNK)
        fields = []
        for ref in (values0_ref, values1_ref):
            block = ref[pl.ds(pl.multiple_of(start * rows, rows), CHUNK * rows), :]
            fields.append(
                jnp.concatenate([block[e * rows : (e + 1) * rows, :] for e in range(CHUNK)], axis=1)
            )
        mixed = bdot(weights, jnp.concatenate(fields, axis=0))
        mixed = (mixed[:rows] + (mixed[rows : 2 * rows] + mixed[2 * rows :])).astype(BF16)
        every = bdot(
            jnp.concatenate([mixed[:, e * slots : (e + 1) * slots] for e in range(CHUNK)], axis=0),
            push_ref[...],
        )
        pairs = pairs_ref[...]
        for e in range(CHUNK):
            pairs = jnp.where(lane == start + e, every[e * rows : (e + 1) * rows, :], pairs)
        pairs_ref[...] = pairs
        return carry

    lax.fori_loop(0, elems // CHUNK, chunk, 0, unroll=True)
    third = pairs_ref[:, 2 * elems :]
    slip = slip_ref[...].astype(F32)
    grads_ref[0] = -(pairs_ref[:, :elems] + slip * friction_ref[...] * third)
    grads_ref[1] = -pairs_ref[:, elems : 2 * elems]
    grads_ref[2] = -slip * normal_ref[...] * third


def call(kernel, outs, scratch, args, smem=()):
    return pl.pallas_call(
        kernel,
        out_shape=[jax.ShapeDtypeStruct(shape, dtype) for shape, dtype in outs],
        in_specs=[
            pl.BlockSpec(memory_space=pltpu.SMEM if i in smem else pltpu.VMEM)
            for i in range(len(args))
        ],
        out_specs=[pl.BlockSpec(memory_space=pltpu.VMEM) for unused in outs],
        scratch_shapes=[pltpu.VMEM(shape, dtype) for shape, dtype in scratch],
        compiler_params=pltpu.CompilerParams(vmem_limit_bytes=VMEM_LIMIT),
    )(*args)


def exchanged(a, b):
    count = lax.axis_size(AXIS)
    first = [(i, i ^ 1) for i in range(count) if i ^ 1 < count]
    other = [(i, i + 1 if i % 2 else i - 1) for i in range(count)]
    second = [(i, j) for i, j in other if 0 <= j < count]
    return lax.ppermute(a, AXIS, first), lax.ppermute(b, AXIS, second)


def everyones(copies):
    return lax.all_to_all(copies, AXIS, 0, 0, tiled=True)


def total(value):
    count = lax.axis_size(AXIS)
    stride = 1
    while stride < count:
        left = count // stride
        radix = 2 if stride == 1 or left % 4 else 4
        parts = [value]
        for d in range(1, radix):
            route = []
            for i in range(count):
                digit = (i // stride) % radix
                route.append((i, i + ((digit ^ d) - digit) * stride))
            parts.append(lax.ppermute(value, AXIS, route))
        while len(parts) > 1:
            parts = [parts[2 * i] + parts[2 * i + 1] for i in range(len(parts) // 2)]
        value = parts[0]
        stride *= radix
    return value


def on_device(
    sensitivity, diagonal, displacement, connectivity, normal_stiff, shear_stiff, friction, slip_state,
    owner_map, templates,
):
    devices = lax.axis_size(AXIS)
    rows, owned = sensitivity.shape
    depth = owner_map.shape[2]
    elems, slots = connectivity.shape
    width = owned + 2 * depth
    count = width // depth
    part = rows * rows // 128
    extra = -(-count // 16) * 16
    wide = ((rows, width), F32)
    band = ((rows, 2 * depth), F32)
    picked = ((elems * rows, slots), BF16)

    line = lambda array: array[None, :]
    disp, diag = line(displacement), line(diagonal)
    normal, shear, fric, slip = line(normal_stiff), line(shear_stiff), line(friction), line(slip_state)
    owner = owner_map[0]
    stacked = templates.reshape(3 * slots, slots)

    start_band = ((rows + 8, depth), F32)
    gram, a, b, coeffs = call(
        begin_kernel,
        [((devices, part, 128), F32), start_band, start_band, ((3, elems), F32)],
        [],
        [sensitivity, disp, normal, shear, fric, slip],
    )
    a, b = exchanged(a, b)
    gram = everyones(gram)
    basis0, image, a, b, factor0, values0, pushed = call(
        first_kernel,
        [wide, wide, band, band, ((rows, rows), F32), picked, ((slots, 3 * elems), BF16)],
        [((count * rows + extra, depth), BF16), ((count * rows, depth), F32), ((elems, slots), F32)],
        [gram, sensitivity, disp, a, b, diag, connectivity, owner, coeffs, stacked],
        smem=(8,),
    )
    a, b = exchanged(a, b)
    full, gram = call(
        middle_kernel, [wide, ((devices, 2 * part, 128), F32)], [], [basis0, image, a, b]
    )
    gram = everyones(gram)
    basis1, image, a, b, small, values1 = call(
        second_kernel,
        [wide, wide, band, band, ((4, rows, rows), F32), picked],
        [((count * rows, depth), BF16), ((count * rows, depth), F32)],
        [gram, factor0, basis0, full, diag, connectivity, owner, coeffs, stacked],
        smem=(7,),
    )
    a, b = exchanged(a, b)
    gram = call(late_kernel, [((3 * part, 128), F32)], [], [basis0, basis1, image, a, b])[0]
    gram = total(gram)
    adjoint, grads = call(
        last_kernel,
        [((rows, owned), F32), ((3, rows, elems), F32)],
        [((rows, 3 * elems), F32)],
        [gram, factor0, small, basis0, basis1, values0, values1, pushed, normal, fric, slip],
    )
    return adjoint, grads


def solution(mesh):
    in_specs = (
        P(None, "brick"),
        P("brick"),
        P("brick"),
        P("brick", None),
        P("brick"),
        P("brick"),
        P("brick"),
        P("brick"),
        P("brick", None, None),
        P(),
    )
    out_specs = (P(None, "brick"), P(None, None, "brick"))
    return jax.shard_map(
        on_device, mesh=mesh, in_specs=in_specs, out_specs=out_specs, check_vma=False
    )
```

```python
import jax
import jax.numpy as jnp
from jax import lax
from jax.experimental import pallas as pl
from jax.experimental.pallas import tpu as pltpu
from jax.sharding import PartitionSpec as P

CHUNK = 16
PIVOTS = 16
VMEM_LIMIT = 48 * 1024 * 1024
AXIS = "brick"
F32 = jnp.float32
BF16 = jnp.bfloat16
NN = (((1,), (0,)), ((), ()))
NT = (((1,), (1,)), ((), ()))
TN = (((0,), (0,)), ((), ()))


def fdot(a, b, dims=NN):
    return lax.dot_general(a, b, dims, precision=lax.Precision.HIGHEST, preferred_element_type=F32)


def bdot(a, b, dims=NN):
    return lax.dot_general(a, b, dims, preferred_element_type=F32)


def lower_inverse(gram):
    n = gram.shape[0]
    row_id = lax.broadcasted_iota(jnp.int32, (n, n), 0)
    col_id = lax.broadcasted_iota(jnp.int32, (n, n), 1)
    work, side = gram, jnp.where(row_id == col_id, 1.0, 0.0).astype(F32)
    for first in range(0, n, PIVOTS):
        places = range(first, first + PIVOTS)
        cols = [jnp.broadcast_to(work[:, k : k + 1], (n, n)) for k in places]
        rows = [work[k : k + 1, :] for k in places]
        sides = [side[k : k + 1, :] for k in places]
        for j, k in enumerate(places):
            step = jnp.where(row_id > k, cols[j] * (1.0 / cols[j][k : k + 1, :]), 0.0)
            for m in range(j + 1, PIVOTS):
                at = first + m
                cols[m] = cols[m] - step * cols[j][at : at + 1, :]
                rows[m] = rows[m] - step[at : at + 1, :] * rows[j]
                sides[m] = sides[m] - step[at : at + 1, :] * sides[j]
            work = work - step * rows[j]
            side = side - step * sides[j]
    diag = jnp.sum(jnp.where(row_id == col_id, work, 0.0), axis=1, keepdims=True)
    scale = 1.0 / jnp.sqrt(diag)
    return side * scale, jnp.where(col_id >= row_id, work, 0.0) * scale


def packed(square):
    n = square.shape[0]
    fold = 128 // n
    part = n // fold
    return jnp.concatenate([square[j * part : (j + 1) * part, :] for j in range(fold)], axis=1)


def unpacked(tile):
    n = int((tile.shape[0] * 128) ** 0.5)
    fold = 128 // n
    return jnp.concatenate([tile[:, j * n : (j + 1) * n] for j in range(fold)], axis=0)


def tall(row, count):
    return jnp.broadcast_to(row, (count, row.shape[1])).astype(BF16)


def one_hot(lo_rows, depth):
    slots = lo_rows.shape[1]
    place = lax.broadcasted_iota(jnp.int32, (depth, slots), 0).astype(F32).astype(BF16)
    one, zero = jnp.ones((), BF16), jnp.zeros((), BF16)
    return jnp.concatenate(
        [
            jnp.where(place == tall(lo_rows[e : e + 1, :], depth), one, zero)
            for e in range(lo_rows.shape[0])
        ],
        axis=1,
    )


def coefficients(joint_refs, element):
    normal, shear, friction, slip = (ref[element] for ref in joint_refs)
    return normal, shear, slip.astype(F32) * friction * normal


def apply_elements(
    half, conn_ref, owner_ref, joint_refs, stacked_ref, values_ref, tiles_ref, total_ref,
    state=None, state_ref=None,
):
    rows, width = half.shape
    depth = owner_ref.shape[1]
    count = width // depth
    elems, slots = conn_ref.shape
    owner = owner_ref[...].astype(F32)
    below, above = one_hot(owner[0:1, :], depth), one_hot(owner[1:2, :], depth)
    tiles_ref[:rows, :] = bdot(half[:, :depth], below).astype(BF16)
    for h in range(1, count - 1):
        tiles_ref[h * rows : (h + 1) * rows, :] = half[:, h * depth : (h + 1) * depth]
    tiles_ref[(count - 1) * rows : count * rows, :] = bdot(half[:, width - depth :], above).astype(BF16)
    if state is not None:
        extra = tiles_ref.shape[0] - count * rows
        pieces = [state[:, h * depth : (h + 1) * depth] for h in range(count)]
        pieces[0] = bdot(tall(pieces[0], 16), below)[0:1, :]
        pieces[-1] = bdot(tall(pieces[-1], 16), above)[0:1, :]
        pieces.append(jnp.zeros((extra - count, depth), F32))
        tiles_ref[count * rows :, :] = jnp.concatenate(pieces, axis=0).astype(BF16)
    total_ref[...] = jnp.zeros_like(total_ref)
    zero = jnp.zeros((), BF16)

    def chunk(step, carry):
        start = pl.multiple_of(step * CHUNK, CHUNK)
        conn = conn_ref[pl.ds(start, CHUNK), :]
        hi = lax.div(conn, depth)
        hot = one_hot((conn - hi * depth).astype(F32), depth)
        spread = bdot(tiles_ref[...], hot)
        hi_wide = [tall(hi[e : e + 1, :].astype(F32), rows) for e in range(CHUNK)]
        scaled = []
        for e in range(CHUNK):
            here = slice(e * slots, (e + 1) * slots)
            value = spread[:rows, here]
            for h in range(1, count):
                value = jnp.where(
                    hi[e : e + 1, :] == h, spread[h * rows : (h + 1) * rows, here], value
                )
            values_ref[pl.ds(pl.multiple_of((start + e) * rows, rows), rows), :] = value.astype(BF16)
            scaled.append(
                jnp.concatenate(
                    [(value * coeff).astype(BF16) for coeff in coefficients(joint_refs, start + e)],
                    axis=1,
                )
            )
            if state is not None:
                picked = spread[count * rows :, here]
                match = lax.broadcasted_iota(jnp.int32, picked.shape, 0) == hi[e : e + 1, :]
                state_ref[pl.ds(start + e, 1), :] = jnp.sum(
                    jnp.where(match, picked, 0.0), axis=0, keepdims=True
                )
        result = bdot(jnp.concatenate(scaled, axis=0), stacked_ref[...]).astype(BF16)
        masked = jnp.concatenate(
            [
                jnp.concatenate(
                    [
                        jnp.where(
                            hi_wide[e] == jnp.full((), h, BF16),
                            result[e * rows : (e + 1) * rows, :],
                            zero,
                        )
                        for e in range(CHUNK)
                    ],
                    axis=1,
                )
                for h in range(count)
            ],
            axis=0,
        )
        total_ref[...] += bdot(masked, hot, NT)
        return carry

    lax.fori_loop(0, elems // CHUNK, chunk, 0, unroll=True)
    parts = [total_ref[h * rows : (h + 1) * rows, :] for h in range(count)]
    for at, match in ((0, below), (count - 1, above)):
        top = parts[at].astype(BF16)
        rest = (parts[at] - top.astype(F32)).astype(BF16)
        both = bdot(jnp.concatenate([top, rest], axis=0), match, NT)
        parts[at] = both[:rows] + both[rows:]
    return parts


def send_bands(low, high, a_ref, b_ref):
    odd = lax.axis_index(AXIS) % 2 == 1
    a_ref[...] = jnp.where(odd, low, high)
    b_ref[...] = jnp.where(odd, high, low)


def received_bands(a_ref, b_ref):
    odd = lax.axis_index(AXIS) % 2 == 1
    a, b = a_ref[...], b_ref[...]
    return jnp.where(odd, a, b), jnp.where(odd, b, a)


def write_image(basis, parts, diag_ref, image_ref, a_ref, b_ref, state=None):
    rows, width = basis.shape
    depth = parts[0].shape[1]
    me = lax.axis_index(AXIS)
    low = parts[0] * jnp.where(me == 0, 0.0, 1.0)
    high = parts[-1] * jnp.where(me == lax.axis_size(AXIS) - 1, 0.0, 1.0)
    own = [
        diag_ref[:, (h - 1) * depth : h * depth] * basis[:, h * depth : (h + 1) * depth] + parts[h]
        for h in range(1, len(parts) - 1)
    ]
    image_ref[...] = jnp.concatenate([low] + own + [high], axis=1)
    bands = [jnp.concatenate([own[0], low], axis=1), jnp.concatenate([own[-1], high], axis=1)]
    if state is not None:
        spare = jnp.zeros((a_ref.shape[0] - rows - 1, 2 * depth), F32)
        bands = [
            jnp.concatenate([band, row, spare], axis=0)
            for band, row in zip(bands, (state[:, : 2 * depth], state[:, -2 * depth :]))
        ]
    send_bands(*bands, a_ref, b_ref)


def complete(image_ref, low, high):
    rows, width = image_ref.shape
    depth = low.shape[1] // 2
    low, high = low[:rows], high[:rows]
    return jnp.concatenate(
        [
            image_ref[:, : 2 * depth] + low,
            image_ref[:, 2 * depth : width - 2 * depth],
            image_ref[:, width - 2 * depth :] + jnp.concatenate([high[:, depth:], high[:, :depth]], axis=1),
        ],
        axis=1,
    )


def begin_kernel(sens_ref, owner_in, gram_ref, a_ref, b_ref, owner_ref, sem):
    copy = pltpu.make_async_copy(owner_in, owner_ref, sem)
    copy.start()
    sens = sens_ref[...]
    depth = a_ref.shape[1]
    owned = sens.shape[1]
    gram = packed(fdot(sens, sens, NT))
    gram_ref[...] = jnp.broadcast_to(gram[None], gram_ref.shape)
    send_bands(sens[:, :depth], sens[:, owned - depth :], a_ref, b_ref)
    copy.wait()


def first_kernel(
    gram_ref, sens_ref, disp_ref, a_in, b_in, diag_ref, conn_ref, owner_ref, stacked_ref,
    normal_ref, shear_ref, friction_ref, slip_ref,
    basis_ref, image_ref, a_ref, b_ref, factor_ref, values_ref, tiles_ref, total_ref,
):
    inverse, factor = lower_inverse(unpacked(jnp.sum(gram_ref[...], axis=0)))
    factor_ref[...] = factor
    low, high = received_bands(a_in, b_in)
    basis = fdot(inverse, jnp.concatenate([low, sens_ref[...], high], axis=1))
    basis_ref[...] = basis
    parts = apply_elements(
        basis.astype(BF16), conn_ref, owner_ref, (normal_ref, shear_ref, friction_ref, slip_ref),
        stacked_ref, values_ref, tiles_ref, total_ref,
    )
    write_image(basis, parts, diag_ref, image_ref, a_ref, b_ref, disp_ref[...].astype(F32))


def own_part(field, depth):
    return field[:, depth : field.shape[1] - depth]


def middle_kernel(basis_ref, image_ref, disp_ref, a_in, b_in, full_ref, state_ref, gram_ref):
    depth = a_in.shape[1] // 2
    low, high = received_bands(a_in, b_in)
    full = complete(image_ref, low, high)
    at = full.shape[0]
    state_ref[...] = jnp.concatenate(
        [low[at : at + 1, depth:], disp_ref[...].astype(F32), high[at : at + 1, :depth]], axis=1
    )
    full_ref[...] = full
    own = own_part(full, depth)
    rows = own.shape[0]
    both = fdot(jnp.concatenate([own_part(basis_ref[...], depth), own], axis=0), own, NT)
    tile = jnp.concatenate([packed(both[:rows]), packed(both[rows:])], axis=0)
    gram_ref[...] = jnp.broadcast_to(tile[None], gram_ref.shape)


def second_kernel(
    gram_ref, factor0_ref, basis0_ref, full_ref, row_ref, diag_ref, conn_ref, owner_ref, stacked_ref,
    normal_ref, shear_ref, friction_ref, slip_ref,
    basis_ref, image_ref, a_ref, b_ref, small_ref, values_ref, push_ref,
    tiles_ref, total_ref, state_ref,
):
    elems, slots = conn_ref.shape
    tile = jnp.sum(gram_ref[...], axis=0)
    part = tile.shape[0] // 2
    proj, square = unpacked(tile[:part]), unpacked(tile[part:])
    inverse, factor = lower_inverse(square - fdot(proj, proj, TN))
    head, unused = lower_inverse(square)
    reduced = full_ref[...] - fdot(proj, basis0_ref[...], TN)
    basis = fdot(inverse, reduced)
    basis_ref[...] = basis
    small_ref[0] = head
    small_ref[1] = fdot(head, proj, NT)
    small_ref[2] = fdot(head, factor, NT)
    small_ref[3] = fdot(head, fdot(proj, factor0_ref[...], TN))
    parts = apply_elements(
        basis.astype(BF16), conn_ref, owner_ref, (normal_ref, shear_ref, friction_ref, slip_ref),
        stacked_ref, values_ref, tiles_ref, total_ref, row_ref[...], state_ref,
    )
    write_image(basis, parts, diag_ref, image_ref, a_ref, b_ref)
    moved = state_ref[...].astype(BF16)
    for k in range(3):
        push_ref[:, k * elems : (k + 1) * elems] = bdot(
            stacked_ref[k * slots : (k + 1) * slots, :], moved, NT
        ).astype(BF16)


def late_kernel(basis0_ref, basis1_ref, image_ref, a_in, b_in, gram_ref):
    depth = a_in.shape[1] // 2
    own = own_part(complete(image_ref, *received_bands(a_in, b_in)), depth)
    rows = own.shape[0]
    every = fdot(
        jnp.concatenate(
            [own_part(basis0_ref[...], depth), own_part(basis1_ref[...], depth), own], axis=0
        ),
        own,
        NT,
    )
    gram_ref[...] = jnp.concatenate(
        [packed(every[j * rows : (j + 1) * rows]) for j in range(3)], axis=0
    )


def split3(value):
    first = value.astype(BF16)
    rest = value - first.astype(F32)
    second = rest.astype(BF16)
    return jnp.concatenate([first, second, (rest - second.astype(F32)).astype(BF16)], axis=0)


def last_kernel(
    gram_ref, factor0_ref, small_ref, basis0_ref, basis1_ref, values0_ref, values1_ref, push_ref,
    normal_ref, friction_ref, slip_ref, adjoint_ref, grads_ref, pairs_ref,
):
    rows, width = basis0_ref.shape
    depth = (width - adjoint_ref.shape[1]) // 2
    elems = normal_ref.shape[1]
    slots = values0_ref.shape[1]
    part = gram_ref.shape[0] // 3
    p01, p11, n11 = (unpacked(gram_ref[j * part : (j + 1) * part, :]) for j in range(3))
    upper0 = factor0_ref[...]
    head, head_side = small_ref[0], small_ref[3]
    cross = fdot(small_ref[1], p01) + fdot(small_ref[2], p11)
    tail, unused = lower_inverse(n11 - fdot(cross, cross, TN))
    tail_side = fdot(tail, fdot(p01, upper0, TN) - fdot(cross, head_side, TN))
    w1 = fdot(tail, tail_side, TN)
    turned = jnp.concatenate(
        [fdot(head_side - fdot(cross, w1), head, TN), fdot(tail_side, tail, TN)], axis=1
    )
    adjoint_ref[...] = fdot(
        turned,
        jnp.concatenate(
            [own_part(basis0_ref[...], depth), own_part(basis1_ref[...], depth)], axis=0
        ),
    )
    weights = split3(turned)
    pairs_ref[...] = jnp.zeros_like(pairs_ref)
    lane = lax.broadcasted_iota(jnp.int32, (rows, 3 * elems), 1) % elems

    def chunk(step, carry):
        start = pl.multiple_of(step * CHUNK, CHUNK)
        fields = []
        for ref in (values0_ref, values1_ref):
            block = ref[pl.ds(pl.multiple_of(start * rows, rows), CHUNK * rows), :]
            fields.append(
                jnp.concatenate([block[e * rows : (e + 1) * rows, :] for e in range(CHUNK)], axis=1)
            )
        mixed = bdot(weights, jnp.concatenate(fields, axis=0))
        mixed = (mixed[:rows] + (mixed[rows : 2 * rows] + mixed[2 * rows :])).astype(BF16)
        every = bdot(
            jnp.concatenate([mixed[:, e * slots : (e + 1) * slots] for e in range(CHUNK)], axis=0),
            push_ref[...],
        )
        pairs = pairs_ref[...]
        for e in range(CHUNK):
            pairs = jnp.where(lane == start + e, every[e * rows : (e + 1) * rows, :], pairs)
        pairs_ref[...] = pairs
        return carry

    lax.fori_loop(0, elems // CHUNK, chunk, 0, unroll=True)
    third = pairs_ref[:, 2 * elems :]
    slip = slip_ref[...].astype(F32)
    grads_ref[0] = -(pairs_ref[:, :elems] + slip * friction_ref[...] * third)
    grads_ref[1] = -pairs_ref[:, elems : 2 * elems]
    grads_ref[2] = -slip * normal_ref[...] * third


def call(kernel, outs, scratch, args, smem=(), anywhere=()):
    spaces = {i: pltpu.SMEM for i in smem} | {i: pl.ANY for i in anywhere}
    return pl.pallas_call(
        kernel,
        out_shape=[jax.ShapeDtypeStruct(shape, dtype) for shape, dtype in outs],
        in_specs=[
            pl.BlockSpec(memory_space=spaces.get(i, pltpu.VMEM)) for i in range(len(args))
        ],
        out_specs=[pl.BlockSpec(memory_space=pltpu.VMEM) for unused in outs],
        scratch_shapes=[
            pltpu.SemaphoreType.DMA if item is None else pltpu.VMEM(*item) for item in scratch
        ],
        compiler_params=pltpu.CompilerParams(vmem_limit_bytes=VMEM_LIMIT),
    )(*args)


def exchanged(a, b):
    count = lax.axis_size(AXIS)
    first = [(i, i ^ 1) for i in range(count) if i ^ 1 < count]
    other = [(i, i + 1 if i % 2 else i - 1) for i in range(count)]
    second = [(i, j) for i, j in other if 0 <= j < count]
    return lax.ppermute(a, AXIS, first), lax.ppermute(b, AXIS, second)


def everyones(copies):
    return lax.all_to_all(copies, AXIS, 0, 0, tiled=True)


def total(value):
    count = lax.axis_size(AXIS)
    stride = 1
    while stride < count:
        left = count // stride
        radix = 2 if stride == 1 or left % 4 else 4
        parts = [value]
        for d in range(1, radix):
            route = []
            for i in range(count):
                digit = (i // stride) % radix
                route.append((i, i + ((digit ^ d) - digit) * stride))
            parts.append(lax.ppermute(value, AXIS, route))
        while len(parts) > 1:
            parts = [parts[2 * i] + parts[2 * i + 1] for i in range(len(parts) // 2)]
        value = parts[0]
        stride *= radix
    return value


def on_device(
    sensitivity, diagonal, displacement, connectivity, normal_stiff, shear_stiff, friction, slip_state,
    owner_map, templates,
):
    devices = lax.axis_size(AXIS)
    rows, owned = sensitivity.shape
    depth = owner_map.shape[2]
    elems, slots = connectivity.shape
    width = owned + 2 * depth
    count = width // depth
    part = rows * rows // 128
    extra = -(-count // 16) * 16
    wide = ((rows, width), F32)
    band = ((rows, 2 * depth), F32)
    picked = ((elems * rows, slots), BF16)

    line = lambda array: array[None, :]
    disp, diag = line(displacement), line(diagonal)
    normal, fric, slip = line(normal_stiff), line(friction), line(slip_state)
    owner = owner_map[0]
    stacked = templates.reshape(3 * slots, slots)

    joints = [normal_stiff, shear_stiff, friction, slip_state]

    gram, a, b, owner = call(
        begin_kernel,
        [((devices, part, 128), F32), ((rows, depth), F32), ((rows, depth), F32), (owner.shape, owner.dtype)],
        [None],
        [sensitivity, owner],
        anywhere=(1,),
    )
    a, b = exchanged(a, b)
    gram = everyones(gram)
    taller = ((rows + 8, 2 * depth), F32)
    basis0, image, a, b, factor0, values0 = call(
        first_kernel,
        [wide, wide, taller, taller, ((rows, rows), F32), picked],
        [((count * rows, depth), BF16), ((count * rows, depth), F32)],
        [gram, sensitivity, disp, a, b, diag, connectivity, owner, stacked] + joints,
        smem=(9, 10, 11, 12),
    )
    a, b = exchanged(a, b)
    full, state, gram = call(
        middle_kernel,
        [wide, ((1, width), F32), ((devices, 2 * part, 128), F32)],
        [],
        [basis0, image, disp, a, b],
    )
    gram = everyones(gram)
    basis1, image, a, b, small, values1, pushed = call(
        second_kernel,
        [wide, wide, band, band, ((4, rows, rows), F32), picked, ((slots, 3 * elems), BF16)],
        [((count * rows + extra, depth), BF16), ((count * rows, depth), F32), ((elems, slots), F32)],
        [gram, factor0, basis0, full, state, diag, connectivity, owner, stacked] + joints,
        smem=(9, 10, 11, 12),
    )
    a, b = exchanged(a, b)
    gram = call(late_kernel, [((3 * part, 128), F32)], [], [basis0, basis1, image, a, b])[0]
    gram = total(gram)
    adjoint, grads = call(
        last_kernel,
        [((rows, owned), F32), ((3, rows, elems), F32)],
        [((rows, 3 * elems), F32)],
        [gram, factor0, small, basis0, basis1, values0, values1, pushed, normal, fric, slip],
    )
    return adjoint, grads


def solution(mesh):
    in_specs = (
        P(None, "brick"),
        P("brick"),
        P("brick"),
        P("brick", None),
        P("brick"),
        P("brick"),
        P("brick"),
        P("brick"),
        P("brick", None, None),
        P(),
    )
    out_specs = (P(None, "brick"), P(None, None, "brick"))
    return jax.shard_map(
        on_device, mesh=mesh, in_specs=in_specs, out_specs=out_specs, check_vma=False
    )
```

```python
import jax
import jax.numpy as jnp
from jax import lax
from jax.experimental import pallas as pl
from jax.experimental.pallas import tpu as pltpu
from jax.sharding import PartitionSpec as P

CHUNK = 16
PIVOTS = 16
VMEM_LIMIT = 48 * 1024 * 1024
AXIS = "brick"
F32 = jnp.float32
BF16 = jnp.bfloat16
NN = (((1,), (0,)), ((), ()))
NT = (((1,), (1,)), ((), ()))
TN = (((0,), (0,)), ((), ()))


def fdot(a, b, dims=NN):
    return lax.dot_general(a, b, dims, precision=lax.Precision.HIGHEST, preferred_element_type=F32)


def bdot(a, b, dims=NN):
    return lax.dot_general(a, b, dims, preferred_element_type=F32)


def lower_inverse(gram):
    n = gram.shape[0]
    row_id = lax.broadcasted_iota(jnp.int32, (n, n), 0)
    col_id = lax.broadcasted_iota(jnp.int32, (n, n), 1)
    work, side = gram, jnp.where(row_id == col_id, 1.0, 0.0).astype(F32)
    for first in range(0, n, PIVOTS):
        places = range(first, first + PIVOTS)
        cols = [jnp.broadcast_to(work[:, k : k + 1], (n, n)) for k in places]
        rows = [work[k : k + 1, :] for k in places]
        sides = [side[k : k + 1, :] for k in places]
        for j, k in enumerate(places):
            step = jnp.where(row_id > k, cols[j] * (1.0 / cols[j][k : k + 1, :]), 0.0)
            for m in range(j + 1, PIVOTS):
                at = first + m
                cols[m] = cols[m] - step * cols[j][at : at + 1, :]
                rows[m] = rows[m] - step[at : at + 1, :] * rows[j]
                sides[m] = sides[m] - step[at : at + 1, :] * sides[j]
            work = work - step * rows[j]
            side = side - step * sides[j]
    diag = jnp.sum(jnp.where(row_id == col_id, work, 0.0), axis=1, keepdims=True)
    scale = 1.0 / jnp.sqrt(diag)
    return side * scale, jnp.where(col_id >= row_id, work, 0.0) * scale


def packed(square):
    n = square.shape[0]
    fold = 128 // n
    part = n // fold
    return jnp.concatenate([square[j * part : (j + 1) * part, :] for j in range(fold)], axis=1)


def unpacked(tile):
    n = int((tile.shape[0] * 128) ** 0.5)
    fold = 128 // n
    return jnp.concatenate([tile[:, j * n : (j + 1) * n] for j in range(fold)], axis=0)


def tall(row, count):
    return jnp.broadcast_to(row, (count, row.shape[1])).astype(BF16)


def one_hot(lo_rows, depth):
    slots = lo_rows.shape[1]
    place = lax.broadcasted_iota(jnp.int32, (depth, slots), 0).astype(F32).astype(BF16)
    one, zero = jnp.ones((), BF16), jnp.zeros((), BF16)
    return jnp.concatenate(
        [
            jnp.where(place == tall(lo_rows[e : e + 1, :], depth), one, zero)
            for e in range(lo_rows.shape[0])
        ],
        axis=1,
    )


def apply_elements(
    half, conn_ref, owner_ref, coeff_ref, stacked_ref, values_ref, tiles_ref, total_ref,
    state=None, state_ref=None,
):
    rows, width = half.shape
    depth = owner_ref.shape[1]
    count = width // depth
    elems, slots = conn_ref.shape
    owner = owner_ref[...]
    below, above = one_hot(owner[0:1, :], depth), one_hot(owner[1:2, :], depth)
    tiles_ref[:rows, :] = bdot(half[:, :depth], below).astype(BF16)
    for h in range(1, count - 1):
        tiles_ref[h * rows : (h + 1) * rows, :] = half[:, h * depth : (h + 1) * depth]
    tiles_ref[(count - 1) * rows : count * rows, :] = bdot(half[:, width - depth :], above).astype(BF16)
    if state is not None:
        extra = tiles_ref.shape[0] - count * rows
        pieces = [state[:, h * depth : (h + 1) * depth] for h in range(count)]
        pieces[0] = bdot(tall(pieces[0], 16), below)[0:1, :]
        pieces[-1] = bdot(tall(pieces[-1], 16), above)[0:1, :]
        pieces.append(jnp.zeros((extra - count, depth), F32))
        tiles_ref[count * rows :, :] = jnp.concatenate(pieces, axis=0).astype(BF16)
    total_ref[...] = jnp.zeros_like(total_ref)
    zero = jnp.zeros((), BF16)

    def chunk(step, carry):
        start = pl.multiple_of(step * CHUNK, CHUNK)
        conn = conn_ref[pl.ds(start, CHUNK), :]
        hi = lax.div(conn, depth)
        hot = one_hot((conn - hi * depth).astype(F32), depth)
        spread = bdot(tiles_ref[...], hot)
        hi_wide = [tall(hi[e : e + 1, :].astype(F32), rows) for e in range(CHUNK)]
        scaled = []
        for e in range(CHUNK):
            here = slice(e * slots, (e + 1) * slots)
            value = spread[:rows, here]
            for h in range(1, count):
                value = jnp.where(
                    hi[e : e + 1, :] == h, spread[h * rows : (h + 1) * rows, here], value
                )
            values_ref[pl.ds(pl.multiple_of((start + e) * rows, rows), rows), :] = value.astype(BF16)
            scaled.append(
                jnp.concatenate(
                    [(value * coeff_ref[k, start + e]).astype(BF16) for k in range(3)], axis=1
                )
            )
            if state is not None:
                picked = spread[count * rows :, here]
                match = lax.broadcasted_iota(jnp.int32, picked.shape, 0) == hi[e : e + 1, :]
                state_ref[pl.ds(start + e, 1), :] = jnp.sum(
                    jnp.where(match, picked, 0.0), axis=0, keepdims=True
                )
        result = bdot(jnp.concatenate(scaled, axis=0), stacked_ref[...]).astype(BF16)
        masked = jnp.concatenate(
            [
                jnp.concatenate(
                    [
                        jnp.where(
                            hi_wide[e] == jnp.full((), h, BF16),
                            result[e * rows : (e + 1) * rows, :],
                            zero,
                        )
                        for e in range(CHUNK)
                    ],
                    axis=1,
                )
                for h in range(count)
            ],
            axis=0,
        )
        total_ref[...] += bdot(masked, hot, NT)
        return carry

    lax.fori_loop(0, elems // CHUNK, chunk, 0, unroll=True)
    parts = [total_ref[h * rows : (h + 1) * rows, :] for h in range(count)]
    for at, match in ((0, below), (count - 1, above)):
        top = parts[at].astype(BF16)
        rest = (parts[at] - top.astype(F32)).astype(BF16)
        both = bdot(jnp.concatenate([top, rest], axis=0), match, NT)
        parts[at] = both[:rows] + both[rows:]
    return parts


def send_bands(low, high, a_ref, b_ref):
    odd = lax.axis_index(AXIS) % 2 == 1
    a_ref[...] = jnp.where(odd, low, high)
    b_ref[...] = jnp.where(odd, high, low)


def received_bands(a_ref, b_ref):
    odd = lax.axis_index(AXIS) % 2 == 1
    a, b = a_ref[...], b_ref[...]
    return jnp.where(odd, a, b), jnp.where(odd, b, a)


def write_image(basis, parts, diag_ref, image_ref, a_ref, b_ref, state=None):
    rows, width = basis.shape
    depth = parts[0].shape[1]
    me = lax.axis_index(AXIS)
    low = parts[0] * jnp.where(me == 0, 0.0, 1.0)
    high = parts[-1] * jnp.where(me == lax.axis_size(AXIS) - 1, 0.0, 1.0)
    own = [
        diag_ref[:, (h - 1) * depth : h * depth] * basis[:, h * depth : (h + 1) * depth] + parts[h]
        for h in range(1, len(parts) - 1)
    ]
    image_ref[...] = jnp.concatenate([low] + own + [high], axis=1)
    bands = [jnp.concatenate([own[0], low], axis=1), jnp.concatenate([own[-1], high], axis=1)]
    if state is not None:
        spare = jnp.zeros((a_ref.shape[0] - rows - 1, 2 * depth), F32)
        bands = [
            jnp.concatenate([band, row, spare], axis=0)
            for band, row in zip(bands, (state[:, : 2 * depth], state[:, -2 * depth :]))
        ]
    send_bands(*bands, a_ref, b_ref)


def complete(image_ref, low, high):
    rows, width = image_ref.shape
    depth = low.shape[1] // 2
    low, high = low[:rows], high[:rows]
    return jnp.concatenate(
        [
            image_ref[:, : 2 * depth] + low,
            image_ref[:, 2 * depth : width - 2 * depth],
            image_ref[:, width - 2 * depth :] + jnp.concatenate([high[:, depth:], high[:, :depth]], axis=1),
        ],
        axis=1,
    )


def begin_kernel(sens_ref, gram_ref, a_ref, b_ref):
    sens = sens_ref[...]
    depth = a_ref.shape[1]
    owned = sens.shape[1]
    gram = packed(fdot(sens, sens, NT))
    gram_ref[...] = jnp.broadcast_to(gram[None], gram_ref.shape)
    send_bands(sens[:, :depth], sens[:, owned - depth :], a_ref, b_ref)


def first_kernel(
    gram_ref, sens_ref, disp_ref, a_in, b_in, diag_ref, conn_ref, owner_ref, coeff_ref,
    stacked_ref,
    basis_ref, image_ref, a_ref, b_ref, factor_ref, values_ref, tiles_ref, total_ref,
):
    inverse, factor = lower_inverse(unpacked(jnp.sum(gram_ref[...], axis=0)))
    factor_ref[...] = factor
    low, high = received_bands(a_in, b_in)
    basis = fdot(inverse, jnp.concatenate([low, sens_ref[...], high], axis=1))
    basis_ref[...] = basis
    parts = apply_elements(
        basis.astype(BF16), conn_ref, owner_ref, coeff_ref,
        stacked_ref, values_ref, tiles_ref, total_ref,
    )
    write_image(basis, parts, diag_ref, image_ref, a_ref, b_ref, disp_ref[...])


def own_part(field, depth):
    return field[:, depth : field.shape[1] - depth]


def middle_kernel(basis_ref, image_ref, disp_ref, a_in, b_in, full_ref, state_ref, gram_ref):
    depth = a_in.shape[1] // 2
    low, high = received_bands(a_in, b_in)
    full = complete(image_ref, low, high)
    at = full.shape[0]
    state_ref[...] = jnp.concatenate(
        [low[at : at + 1, depth:], disp_ref[...], high[at : at + 1, :depth]], axis=1
    )
    full_ref[...] = full
    own = own_part(full, depth)
    rows = own.shape[0]
    both = fdot(jnp.concatenate([own_part(basis_ref[...], depth), own], axis=0), own, NT)
    tile = jnp.concatenate([packed(both[:rows]), packed(both[rows:])], axis=0)
    gram_ref[...] = jnp.broadcast_to(tile[None], gram_ref.shape)


def second_kernel(
    gram_ref, factor0_ref, basis0_ref, full_ref, row_ref, diag_ref, conn_ref, owner_ref, coeff_ref,
    stacked_ref,
    basis_ref, image_ref, a_ref, b_ref, small_ref, values_ref, push_ref,
    tiles_ref, total_ref, state_ref,
):
    elems, slots = conn_ref.shape
    tile = jnp.sum(gram_ref[...], axis=0)
    part = tile.shape[0] // 2
    proj, square = unpacked(tile[:part]), unpacked(tile[part:])
    inverse, factor = lower_inverse(square - fdot(proj, proj, TN))
    head, unused = lower_inverse(square)
    reduced = full_ref[...] - fdot(proj, basis0_ref[...], TN)
    basis = fdot(inverse, reduced)
    basis_ref[...] = basis
    small_ref[0] = head
    small_ref[1] = fdot(head, proj, NT)
    small_ref[2] = fdot(head, factor, NT)
    small_ref[3] = fdot(head, fdot(proj, factor0_ref[...], TN))
    parts = apply_elements(
        basis.astype(BF16), conn_ref, owner_ref, coeff_ref,
        stacked_ref, values_ref, tiles_ref, total_ref, row_ref[...], state_ref,
    )
    write_image(basis, parts, diag_ref, image_ref, a_ref, b_ref)
    moved = state_ref[...].astype(BF16)
    for k in range(3):
        push_ref[:, k * elems : (k + 1) * elems] = bdot(
            stacked_ref[k * slots : (k + 1) * slots, :], moved, NT
        ).astype(BF16)


def late_kernel(basis0_ref, basis1_ref, image_ref, a_in, b_in, gram_ref):
    depth = a_in.shape[1] // 2
    own = own_part(complete(image_ref, *received_bands(a_in, b_in)), depth)
    rows = own.shape[0]
    every = fdot(
        jnp.concatenate(
            [own_part(basis0_ref[...], depth), own_part(basis1_ref[...], depth), own], axis=0
        ),
        own,
        NT,
    )
    gram_ref[...] = jnp.concatenate(
        [packed(every[j * rows : (j + 1) * rows]) for j in range(3)], axis=0
    )


def split3(value):
    first = value.astype(BF16)
    rest = value - first.astype(F32)
    second = rest.astype(BF16)
    return jnp.concatenate([first, second, (rest - second.astype(F32)).astype(BF16)], axis=0)


def last_kernel(
    gram_ref, factor0_ref, small_ref, basis0_ref, basis1_ref, values0_ref, values1_ref, push_ref,
    normal_ref, friction_ref, slip_ref, adjoint_ref, grads_ref, pairs_ref,
):
    rows, width = basis0_ref.shape
    depth = (width - adjoint_ref.shape[1]) // 2
    elems = normal_ref.shape[1]
    slots = values0_ref.shape[1]
    part = gram_ref.shape[0] // 3
    p01, p11, n11 = (unpacked(gram_ref[j * part : (j + 1) * part, :]) for j in range(3))
    upper0 = factor0_ref[...]
    head, head_side = small_ref[0], small_ref[3]
    cross = fdot(small_ref[1], p01) + fdot(small_ref[2], p11)
    tail, unused = lower_inverse(n11 - fdot(cross, cross, TN))
    tail_side = fdot(tail, fdot(p01, upper0, TN) - fdot(cross, head_side, TN))
    w1 = fdot(tail, tail_side, TN)
    turned = jnp.concatenate(
        [fdot(head_side - fdot(cross, w1), head, TN), fdot(tail_side, tail, TN)], axis=1
    )
    adjoint_ref[...] = fdot(
        turned,
        jnp.concatenate(
            [own_part(basis0_ref[...], depth), own_part(basis1_ref[...], depth)], axis=0
        ),
    )
    weights = split3(turned)
    pairs_ref[...] = jnp.zeros_like(pairs_ref)
    lane = lax.broadcasted_iota(jnp.int32, (rows, 3 * elems), 1) % elems

    def chunk(step, carry):
        start = pl.multiple_of(step * CHUNK, CHUNK)
        fields = []
        for ref in (values0_ref, values1_ref):
            block = ref[pl.ds(pl.multiple_of(start * rows, rows), CHUNK * rows), :]
            fields.append(
                jnp.concatenate([block[e * rows : (e + 1) * rows, :] for e in range(CHUNK)], axis=1)
            )
        mixed = bdot(weights, jnp.concatenate(fields, axis=0))
        mixed = (mixed[:rows] + (mixed[rows : 2 * rows] + mixed[2 * rows :])).astype(BF16)
        every = bdot(
            jnp.concatenate([mixed[:, e * slots : (e + 1) * slots] for e in range(CHUNK)], axis=0),
            push_ref[...],
        )
        pairs = pairs_ref[...]
        for e in range(CHUNK):
            pairs = jnp.where(lane == start + e, every[e * rows : (e + 1) * rows, :], pairs)
        pairs_ref[...] = pairs
        return carry

    lax.fori_loop(0, elems // CHUNK, chunk, 0, unroll=True)
    third = pairs_ref[:, 2 * elems :]
    slip = slip_ref[...].astype(F32)
    grads_ref[0] = -(pairs_ref[:, :elems] + slip * friction_ref[...] * third)
    grads_ref[1] = -pairs_ref[:, elems : 2 * elems]
    grads_ref[2] = -slip * normal_ref[...] * third


def call(kernel, outs, scratch, args, smem=()):
    return pl.pallas_call(
        kernel,
        out_shape=[jax.ShapeDtypeStruct(shape, dtype) for shape, dtype in outs],
        in_specs=[
            pl.BlockSpec(memory_space=pltpu.SMEM if i in smem else pltpu.VMEM)
            for i in range(len(args))
        ],
        out_specs=[pl.BlockSpec(memory_space=pltpu.VMEM) for unused in outs],
        scratch_shapes=[pltpu.VMEM(shape, dtype) for shape, dtype in scratch],
        compiler_params=pltpu.CompilerParams(vmem_limit_bytes=VMEM_LIMIT),
    )(*args)


def exchanged(a, b):
    count = lax.axis_size(AXIS)
    first = [(i, i ^ 1) for i in range(count) if i ^ 1 < count]
    other = [(i, i + 1 if i % 2 else i - 1) for i in range(count)]
    second = [(i, j) for i, j in other if 0 <= j < count]
    return lax.ppermute(a, AXIS, first), lax.ppermute(b, AXIS, second)


def everyones(copies):
    return lax.all_to_all(copies, AXIS, 0, 0, tiled=True)


def total(value):
    count = lax.axis_size(AXIS)
    stride = 1
    while stride < count:
        left = count // stride
        radix = 2 if stride == 1 or left % 4 else 4
        parts = [value]
        for d in range(1, radix):
            route = []
            for i in range(count):
                digit = (i // stride) % radix
                route.append((i, i + ((digit ^ d) - digit) * stride))
            parts.append(lax.ppermute(value, AXIS, route))
        while len(parts) > 1:
            parts = [parts[2 * i] + parts[2 * i + 1] for i in range(len(parts) // 2)]
        value = parts[0]
        stride *= radix
    return value


def on_device(
    sensitivity, diagonal, displacement, connectivity, normal_stiff, shear_stiff, friction, slip_state,
    owner_map, templates,
):
    devices = lax.axis_size(AXIS)
    rows, owned = sensitivity.shape
    depth = owner_map.shape[2]
    elems, slots = connectivity.shape
    width = owned + 2 * depth
    count = width // depth
    part = rows * rows // 128
    extra = -(-count // 16) * 16
    wide = ((rows, width), F32)
    band = ((rows, 2 * depth), F32)
    picked = ((elems * rows, slots), BF16)

    line = lambda array: array[None, :]
    disp, diag = line(displacement.astype(F32)), line(diagonal)
    normal, fric, slip = line(normal_stiff), line(friction), line(slip_state)
    owner = owner_map[0].astype(F32)
    stacked = templates.reshape(3 * slots, slots)

    coeffs = jnp.stack([normal_stiff, shear_stiff, slip_state.astype(F32) * friction * normal_stiff])

    gram, a, b = call(
        begin_kernel,
        [((devices, part, 128), F32), ((rows, depth), F32), ((rows, depth), F32)],
        [],
        [sensitivity],
    )
    a, b = exchanged(a, b)
    gram = everyones(gram)
    taller = ((rows + 8, 2 * depth), F32)
    basis0, image, a, b, factor0, values0 = call(
        first_kernel,
        [wide, wide, taller, taller, ((rows, rows), F32), picked],
        [((count * rows, depth), BF16), ((count * rows, depth), F32)],
        [gram, sensitivity, disp, a, b, diag, connectivity, owner, coeffs, stacked],
        smem=(8,),
    )
    a, b = exchanged(a, b)
    full, state, gram = call(
        middle_kernel,
        [wide, ((1, width), F32), ((devices, 2 * part, 128), F32)],
        [],
        [basis0, image, disp, a, b],
    )
    gram = everyones(gram)
    basis1, image, a, b, small, values1, pushed = call(
        second_kernel,
        [wide, wide, band, band, ((4, rows, rows), F32), picked, ((slots, 3 * elems), BF16)],
        [((count * rows + extra, depth), BF16), ((count * rows, depth), F32), ((elems, slots), F32)],
        [gram, factor0, basis0, full, state, diag, connectivity, owner, coeffs, stacked],
        smem=(8,),
    )
    a, b = exchanged(a, b)
    gram = call(late_kernel, [((3 * part, 128), F32)], [], [basis0, basis1, image, a, b])[0]
    gram = total(gram)
    adjoint, grads = call(
        last_kernel,
        [((rows, owned), F32), ((3, rows, elems), F32)],
        [((rows, 3 * elems), F32)],
        [gram, factor0, small, basis0, basis1, values0, values1, pushed, normal, fric, slip],
    )
    return adjoint, grads


def solution(mesh):
    in_specs = (
        P(None, "brick"),
        P("brick"),
        P("brick"),
        P("brick", None),
        P("brick"),
        P("brick"),
        P("brick"),
        P("brick"),
        P("brick", None, None),
        P(),
    )
    out_specs = (P(None, "brick"), P(None, None, "brick"))
    return jax.shard_map(
        on_device, mesh=mesh, in_specs=in_specs, out_specs=out_specs, check_vma=False
    )
```

```python
import jax
import jax.numpy as jnp
from jax import lax
from jax.experimental import pallas as pl
from jax.experimental.pallas import tpu as pltpu
from jax.sharding import PartitionSpec as P

PARTS = 2
CHUNK = 16
PIVOTS = 16
VMEM_LIMIT = 48 * 1024 * 1024
AXIS = "brick"
F32 = jnp.float32
BF16 = jnp.bfloat16
NN = (((1,), (0,)), ((), ()))
NT = (((1,), (1,)), ((), ()))
TN = (((0,), (0,)), ((), ()))


def fdot(a, b, dims=NN):
    return lax.dot_general(a, b, dims, precision=lax.Precision.HIGHEST, preferred_element_type=F32)


def bdot(a, b, dims=NN):
    return lax.dot_general(a, b, dims, preferred_element_type=F32)


def lower_inverse(gram):
    n = gram.shape[0]
    row_id = lax.broadcasted_iota(jnp.int32, (n, n), 0)
    col_id = lax.broadcasted_iota(jnp.int32, (n, n), 1)
    work, side = gram, jnp.where(row_id == col_id, 1.0, 0.0).astype(F32)
    for first in range(0, n, PIVOTS):
        places = range(first, first + PIVOTS)
        cols = [jnp.broadcast_to(work[:, k : k + 1], (n, n)) for k in places]
        rows = [work[k : k + 1, :] for k in places]
        sides = [side[k : k + 1, :] for k in places]
        for j, k in enumerate(places):
            step = jnp.where(row_id > k, cols[j] * (1.0 / cols[j][k : k + 1, :]), 0.0)
            for m in range(j + 1, PIVOTS):
                at = first + m
                cols[m] = cols[m] - step * cols[j][at : at + 1, :]
                rows[m] = rows[m] - step[at : at + 1, :] * rows[j]
                sides[m] = sides[m] - step[at : at + 1, :] * sides[j]
            work = work - step * rows[j]
            side = side - step * sides[j]
    diag = jnp.sum(jnp.where(row_id == col_id, work, 0.0), axis=1, keepdims=True)
    scale = 1.0 / jnp.sqrt(diag)
    return side * scale, jnp.where(col_id >= row_id, work, 0.0) * scale


def packed(square):
    n = square.shape[0]
    fold = 128 // n
    part = n // fold
    return jnp.concatenate([square[j * part : (j + 1) * part, :] for j in range(fold)], axis=1)


def unpacked(tile):
    n = int((tile.shape[0] * 128) ** 0.5)
    fold = 128 // n
    return jnp.concatenate([tile[:, j * n : (j + 1) * n] for j in range(fold)], axis=0)


def packed_symmetric(square):
    n = square.shape[0]
    half = n // 2
    first, second, cross = square[:half, :half], square[half:, half:], square[half:, :half]
    row_id = lax.broadcasted_iota(jnp.int32, (half, half), 0)
    col_id = lax.broadcasted_iota(jnp.int32, (half, half), 1)
    both = jnp.concatenate([jnp.where(row_id >= col_id, first, second), cross], axis=1)
    fold = 128 // n
    part = half // fold
    diag = jnp.sum(jnp.where(row_id == col_id, second, 0.0), axis=0, keepdims=True)
    return jnp.concatenate(
        [
            jnp.concatenate([both[j * part : (j + 1) * part, :] for j in range(fold)], axis=1),
            jnp.concatenate([diag, jnp.zeros((1, 128 - half), F32)], axis=1),
        ],
        axis=0,
    )


def unpacked_symmetric(tile, n):
    half = n // 2
    fold = 128 // n
    part = half // fold
    both = jnp.concatenate([tile[:part, j * n : (j + 1) * n] for j in range(fold)], axis=0)
    same = lax.broadcasted_iota(jnp.int32, (n, n), 0) == lax.broadcasted_iota(jnp.int32, (n, n), 1)
    flipped = fdot(jnp.where(same, 1.0, 0.0).astype(F32), both, NT)
    mixed, cross = both[:, :half], both[:, half:]
    row_id = lax.broadcasted_iota(jnp.int32, (half, half), 0)
    col_id = lax.broadcasted_iota(jnp.int32, (half, half), 1)
    first = jnp.where(row_id >= col_id, mixed, flipped[:half])
    second = jnp.where(row_id < col_id, mixed, flipped[:half])
    second = jnp.where(row_id == col_id, jnp.broadcast_to(tile[part : part + 1, :half], (half, half)), second)
    return jnp.concatenate(
        [
            jnp.concatenate([first, flipped[half:]], axis=1),
            jnp.concatenate([cross, second], axis=1),
        ],
        axis=0,
    )


def tall(row, count):
    return jnp.broadcast_to(row, (count, row.shape[1])).astype(BF16)


def one_hot(lo_rows, depth):
    slots = lo_rows.shape[1]
    place = lax.broadcasted_iota(jnp.int32, (depth, slots), 0).astype(F32).astype(BF16)
    one, zero = jnp.ones((), BF16), jnp.zeros((), BF16)
    return jnp.concatenate(
        [
            jnp.where(place == tall(lo_rows[e : e + 1, :], depth), one, zero)
            for e in range(lo_rows.shape[0])
        ],
        axis=1,
    )


def apply_elements(
    half, conn_ref, owner_ref, coeff_ref, stacked_ref, values_ref, tiles_ref, total_ref,
    state=None, state_ref=None,
):
    rows, width = half.shape
    depth = owner_ref.shape[1]
    count = width // depth
    elems, slots = conn_ref.shape
    owner = owner_ref[...]
    below, above = one_hot(owner[0:1, :], depth), one_hot(owner[1:2, :], depth)
    tiles_ref[:rows, :] = bdot(half[:, :depth], below).astype(BF16)
    for h in range(1, count - 1):
        tiles_ref[h * rows : (h + 1) * rows, :] = half[:, h * depth : (h + 1) * depth]
    tiles_ref[(count - 1) * rows : count * rows, :] = bdot(half[:, width - depth :], above).astype(BF16)
    if state is not None:
        extra = tiles_ref.shape[0] - count * rows
        pieces = [state[:, h * depth : (h + 1) * depth] for h in range(count)]
        pieces[0] = bdot(tall(pieces[0], 16), below)[0:1, :]
        pieces[-1] = bdot(tall(pieces[-1], 16), above)[0:1, :]
        pieces.append(jnp.zeros((extra - count, depth), F32))
        tiles_ref[count * rows :, :] = jnp.concatenate(pieces, axis=0).astype(BF16)
    total_ref[...] = jnp.zeros_like(total_ref)
    zero = jnp.zeros((), BF16)

    def chunk(step, carry):
        start = pl.multiple_of(step * CHUNK, CHUNK)
        conn = conn_ref[pl.ds(start, CHUNK), :]
        hi = lax.div(conn, depth)
        hot = one_hot((conn - hi * depth).astype(F32), depth)
        spread = bdot(tiles_ref[...], hot)
        hi_wide = [tall(hi[e : e + 1, :].astype(F32), rows) for e in range(CHUNK)]
        scaled = []
        for e in range(CHUNK):
            here = slice(e * slots, (e + 1) * slots)
            value = spread[:rows, here]
            for h in range(1, count):
                value = jnp.where(
                    hi[e : e + 1, :] == h, spread[h * rows : (h + 1) * rows, here], value
                )
            values_ref[pl.ds(pl.multiple_of((start + e) * rows, rows), rows), :] = value.astype(BF16)
            scaled.append(
                jnp.concatenate(
                    [(value * coeff_ref[k, start + e]).astype(BF16) for k in range(3)], axis=1
                )
            )
            if state is not None:
                picked = spread[count * rows :, here]
                match = lax.broadcasted_iota(jnp.int32, picked.shape, 0) == hi[e : e + 1, :]
                state_ref[pl.ds(start + e, 1), :] = jnp.sum(
                    jnp.where(match, picked, 0.0), axis=0, keepdims=True
                )
        result = bdot(jnp.concatenate(scaled, axis=0), stacked_ref[...]).astype(BF16)
        masked = jnp.concatenate(
            [
                jnp.concatenate(
                    [
                        jnp.where(
                            hi_wide[e] == jnp.full((), h, BF16),
                            result[e * rows : (e + 1) * rows, :],
                            zero,
                        )
                        for e in range(CHUNK)
                    ],
                    axis=1,
                )
                for h in range(count)
            ],
            axis=0,
        )
        total_ref[...] += bdot(masked, hot, NT)
        return carry

    lax.fori_loop(0, elems // CHUNK, chunk, 0, unroll=True)
    parts = [total_ref[h * rows : (h + 1) * rows, :] for h in range(count)]
    for at, match in ((0, below), (count - 1, above)):
        top = parts[at].astype(BF16)
        rest = (parts[at] - top.astype(F32)).astype(BF16)
        both = bdot(jnp.concatenate([top, rest], axis=0), match, NT)
        parts[at] = both[:rows] + both[rows:]
    return parts


def send_bands(low, high, a_ref, b_ref):
    odd = lax.axis_index(AXIS) % 2 == 1
    a_ref[...] = jnp.where(odd, low, high)
    b_ref[...] = jnp.where(odd, high, low)


def received_bands(a_ref, b_ref):
    odd = lax.axis_index(AXIS) % 2 == 1
    a, b = a_ref[...], b_ref[...]
    return jnp.where(odd, a, b), jnp.where(odd, b, a)


def write_image(basis, parts, diag_ref, image_ref, a_ref, b_ref, state=None):
    rows, width = basis.shape
    depth = parts[0].shape[1]
    me = lax.axis_index(AXIS)
    low = parts[0] * jnp.where(me == 0, 0.0, 1.0)
    high = parts[-1] * jnp.where(me == lax.axis_size(AXIS) - 1, 0.0, 1.0)
    own = [
        diag_ref[:, (h - 1) * depth : h * depth] * basis[:, h * depth : (h + 1) * depth] + parts[h]
        for h in range(1, len(parts) - 1)
    ]
    image_ref[...] = jnp.concatenate([low] + own + [high], axis=1)
    bands = [jnp.concatenate([own[0], low], axis=1), jnp.concatenate([own[-1], high], axis=1)]
    if state is not None:
        spare = jnp.zeros((a_ref.shape[0] - rows - 1, 2 * depth), F32)
        bands = [
            jnp.concatenate([band, row, spare], axis=0)
            for band, row in zip(bands, (state[:, : 2 * depth], state[:, -2 * depth :]))
        ]
    send_bands(*bands, a_ref, b_ref)


def complete(image_ref, low, high):
    rows, width = image_ref.shape
    depth = low.shape[1] // 2
    low, high = low[:rows], high[:rows]
    return jnp.concatenate(
        [
            image_ref[:, : 2 * depth] + low,
            image_ref[:, 2 * depth : width - 2 * depth],
            image_ref[:, width - 2 * depth :] + jnp.concatenate([high[:, depth:], high[:, :depth]], axis=1),
        ],
        axis=1,
    )


def begin_kernel(sens_ref, gram_ref, a_ref, b_ref):
    sens = sens_ref[...]
    depth = a_ref.shape[1]
    owned = sens.shape[1]
    gram = packed(fdot(sens, sens, NT))
    gram_ref[...] = jnp.broadcast_to(gram[None], gram_ref.shape)
    send_bands(sens[:, :depth], sens[:, owned - depth :], a_ref, b_ref)


def first_kernel(
    gram_ref, sens_ref, disp_ref, a_in, b_in, diag_ref, conn_ref, owner_ref, coeff_ref,
    stacked_ref,
    basis_ref, image_ref, a_ref, b_ref, factor_ref, values_ref, tiles_ref, total_ref,
):
    inverse, factor = lower_inverse(unpacked(jnp.sum(gram_ref[...], axis=0)))
    factor_ref[...] = factor
    low, high = received_bands(a_in, b_in)
    basis = fdot(inverse, jnp.concatenate([low, sens_ref[...], high], axis=1))
    basis_ref[...] = basis
    parts = apply_elements(
        basis.astype(BF16), conn_ref, owner_ref, coeff_ref,
        stacked_ref, values_ref, tiles_ref, total_ref,
    )
    write_image(basis, parts, diag_ref, image_ref, a_ref, b_ref, disp_ref[...])


def own_part(field, depth):
    return field[:, depth : field.shape[1] - depth]


def middle_kernel(basis_ref, image_ref, disp_ref, a_in, b_in, full_ref, state_ref, gram_ref):
    depth = a_in.shape[1] // 2
    low, high = received_bands(a_in, b_in)
    full = complete(image_ref, low, high)
    at = full.shape[0]
    state_ref[...] = jnp.concatenate(
        [low[at : at + 1, depth:], disp_ref[...], high[at : at + 1, :depth]], axis=1
    )
    full_ref[...] = full
    own = own_part(full, depth)
    rows = own.shape[0]
    both = fdot(jnp.concatenate([own_part(basis_ref[...], depth), own], axis=0), own, NT)
    tile = jnp.concatenate([packed(both[:rows]), packed_symmetric(both[rows:])], axis=0)
    copies = gram_ref.shape[0]
    for r in range(tile.shape[0]):
        gram_ref[:, r] = jnp.broadcast_to(tile[r : r + 1, :][None], (copies, 1, 128))


def second_kernel(
    gram_ref, factor0_ref, basis0_ref, full_ref, row_ref, diag_ref, conn_ref, owner_ref, coeff_ref,
    stacked_ref,
    basis_ref, image_ref, a_ref, b_ref, small_ref, values_ref, push_ref,
    tiles_ref, total_ref, state_ref,
):
    elems, slots = conn_ref.shape
    summed = jnp.sum(gram_ref[...], axis=0)
    tile = jnp.concatenate([summed[r] for r in range(summed.shape[0])], axis=0)
    n = basis0_ref.shape[0]
    part = n * n // 128
    proj, square = unpacked(tile[:part]), unpacked_symmetric(tile[part:], n)
    inverse, factor = lower_inverse(square - fdot(proj, proj, TN))
    head, unused = lower_inverse(square)
    reduced = full_ref[...] - fdot(proj, basis0_ref[...], TN)
    basis = fdot(inverse, reduced)
    basis_ref[...] = basis
    small_ref[0] = head
    small_ref[1] = fdot(head, proj, NT)
    small_ref[2] = fdot(head, factor, NT)
    small_ref[3] = fdot(head, fdot(proj, factor0_ref[...], TN))
    parts = apply_elements(
        basis.astype(BF16), conn_ref, owner_ref, coeff_ref,
        stacked_ref, values_ref, tiles_ref, total_ref, row_ref[...], state_ref,
    )
    write_image(basis, parts, diag_ref, image_ref, a_ref, b_ref)
    moved = state_ref[...].astype(BF16)
    for k in range(3):
        pushed = bdot(stacked_ref[k * slots : (k + 1) * slots, :], moved, NT).astype(BF16)
        for part in range(PARTS):
            group = elems // PARTS
            push_ref[part, :, k * group : (k + 1) * group] = pushed[:, part * group : (part + 1) * group]


def late_kernel(basis0_ref, basis1_ref, image_ref, a_in, b_in, gram_ref):
    depth = a_in.shape[1] // 2
    own = own_part(complete(image_ref, *received_bands(a_in, b_in)), depth)
    rows = own.shape[0]
    every = fdot(
        jnp.concatenate(
            [own_part(basis0_ref[...], depth), own_part(basis1_ref[...], depth), own], axis=0
        ),
        own,
        NT,
    )
    gram_ref[...] = jnp.concatenate(
        [packed(every[j * rows : (j + 1) * rows]) for j in range(3)], axis=0
    )


def split3(value):
    first = value.astype(BF16)
    rest = value - first.astype(F32)
    second = rest.astype(BF16)
    return jnp.concatenate([first, second, (rest - second.astype(F32)).astype(BF16)], axis=0)


def last_kernel(
    gram_ref, factor0_ref, small_ref, basis0_ref, basis1_ref, values0_ref, values1_ref, push_ref,
    normal_ref, friction_ref, slip_ref, adjoint_ref, grads_ref,
):
    rows, width = basis0_ref.shape
    depth = (width - adjoint_ref.shape[1]) // 2
    elems = normal_ref.shape[1]
    slots = values0_ref.shape[1]
    part = gram_ref.shape[0] // 3
    p01, p11, n11 = (unpacked(gram_ref[j * part : (j + 1) * part, :]) for j in range(3))
    upper0 = factor0_ref[...]
    head, head_side = small_ref[0], small_ref[3]
    cross = fdot(small_ref[1], p01) + fdot(small_ref[2], p11)
    tail, unused = lower_inverse(n11 - fdot(cross, cross, TN))
    tail_side = fdot(tail, fdot(p01, upper0, TN) - fdot(cross, head_side, TN))
    w1_turned = fdot(tail_side, tail, TN)
    w0_turned = fdot(head_side, head, TN) - fdot(w1_turned, fdot(head, cross, TN), NT)
    turned = jnp.concatenate([w0_turned, w1_turned], axis=1)
    adjoint_ref[...] = fdot(
        turned,
        jnp.concatenate(
            [own_part(basis0_ref[...], depth), own_part(basis1_ref[...], depth)], axis=0
        ),
    )
    weights = split3(turned)
    group = elems // PARTS
    lane = lax.broadcasted_iota(jnp.int32, (rows, 3 * group), 1) % group
    found = []
    for part in range(PARTS):
        pairs = jnp.zeros((rows, 3 * group), F32)
        for start in range(part * group, (part + 1) * group, CHUNK):
            fields = []
            for ref in (values0_ref, values1_ref):
                block = ref[start * rows : (start + CHUNK) * rows, :]
                fields.append(
                    jnp.concatenate([block[e * rows : (e + 1) * rows, :] for e in range(CHUNK)], axis=1)
                )
            mixed = bdot(weights, jnp.concatenate(fields, axis=0))
            mixed = (mixed[:rows] + (mixed[rows : 2 * rows] + mixed[2 * rows :])).astype(BF16)
            every = bdot(
                jnp.concatenate([mixed[:, e * slots : (e + 1) * slots] for e in range(CHUNK)], axis=0),
                push_ref[part],
            )
            for e in range(CHUNK):
                at = start - part * group + e
                pairs = jnp.where(lane == at, every[e * rows : (e + 1) * rows, :], pairs)
        found.append(pairs)
    pairs = [
        jnp.concatenate([part[:, k * group : (k + 1) * group] for part in found], axis=1)
        for k in range(3)
    ]
    slip = slip_ref[...].astype(F32)
    grads_ref[0] = -(pairs[0] + slip * friction_ref[...] * pairs[2])
    grads_ref[1] = -pairs[1]
    grads_ref[2] = -slip * normal_ref[...] * pairs[2]


def call(kernel, outs, scratch, args, smem=()):
    return pl.pallas_call(
        kernel,
        out_shape=[jax.ShapeDtypeStruct(shape, dtype) for shape, dtype in outs],
        in_specs=[
            pl.BlockSpec(memory_space=pltpu.SMEM if i in smem else pltpu.VMEM)
            for i in range(len(args))
        ],
        out_specs=[pl.BlockSpec(memory_space=pltpu.VMEM) for unused in outs],
        scratch_shapes=[pltpu.VMEM(shape, dtype) for shape, dtype in scratch],
        compiler_params=pltpu.CompilerParams(vmem_limit_bytes=VMEM_LIMIT),
    )(*args)


def exchanged(a, b):
    count = lax.axis_size(AXIS)
    first = [(i, i ^ 1) for i in range(count) if i ^ 1 < count]
    other = [(i, i + 1 if i % 2 else i - 1) for i in range(count)]
    second = [(i, j) for i, j in other if 0 <= j < count]
    return lax.ppermute(a, AXIS, first), lax.ppermute(b, AXIS, second)


def everyones(copies):
    return lax.all_to_all(copies, AXIS, 0, 0, tiled=True)


def total(value):
    count = lax.axis_size(AXIS)
    stride = 1
    while stride < count:
        left = count // stride
        radix = 2 if stride == 1 or left % 4 else 4
        parts = [value]
        for d in range(1, radix):
            route = []
            for i in range(count):
                digit = (i // stride) % radix
                route.append((i, i + ((digit ^ d) - digit) * stride))
            parts.append(lax.ppermute(value, AXIS, route))
        while len(parts) > 1:
            parts = [parts[2 * i] + parts[2 * i + 1] for i in range(len(parts) // 2)]
        value = parts[0]
        stride *= radix
    return value


def on_device(
    sensitivity, diagonal, displacement, connectivity, normal_stiff, shear_stiff, friction, slip_state,
    owner_map, templates,
):
    devices = lax.axis_size(AXIS)
    rows, owned = sensitivity.shape
    depth = owner_map.shape[2]
    elems, slots = connectivity.shape
    width = owned + 2 * depth
    count = width // depth
    part = rows * rows // 128
    extra = -(-count // 16) * 16
    wide = ((rows, width), F32)
    band = ((rows, 2 * depth), F32)
    picked = ((elems * rows, slots), BF16)

    line = lambda array: array[None, :]
    disp, diag = line(displacement.astype(F32)), line(diagonal)
    normal, fric, slip = line(normal_stiff), line(friction), line(slip_state)
    owner = owner_map[0].astype(F32)
    stacked = templates.reshape(3 * slots, slots)

    coeffs = jnp.stack([normal_stiff, shear_stiff, slip_state.astype(F32) * friction * normal_stiff])

    gram, a, b = call(
        begin_kernel,
        [((devices, part, 128), F32), ((rows, depth), F32), ((rows, depth), F32)],
        [],
        [sensitivity],
    )
    a, b = exchanged(a, b)
    gram = everyones(gram)
    taller = ((rows + 8, 2 * depth), F32)
    basis0, image, a, b, factor0, values0 = call(
        first_kernel,
        [wide, wide, taller, taller, ((rows, rows), F32), picked],
        [((count * rows, depth), BF16), ((count * rows, depth), F32)],
        [gram, sensitivity, disp, a, b, diag, connectivity, owner, coeffs, stacked],
        smem=(8,),
    )
    a, b = exchanged(a, b)
    full, state, gram = call(
        middle_kernel,
        [wide, ((1, width), F32), ((devices, part + part // 2 + 1, 1, 128), F32)],
        [],
        [basis0, image, disp, a, b],
    )
    gram = everyones(gram)
    basis1, image, a, b, small, values1, pushed = call(
        second_kernel,
        [wide, wide, band, band, ((4, rows, rows), F32), picked, ((PARTS, slots, 3 * elems // PARTS), BF16)],
        [((count * rows + extra, depth), BF16), ((count * rows, depth), F32), ((elems, slots), F32)],
        [gram, factor0, basis0, full, state, diag, connectivity, owner, coeffs, stacked],
        smem=(8,),
    )
    a, b = exchanged(a, b)
    gram = call(late_kernel, [((3 * part, 128), F32)], [], [basis0, basis1, image, a, b])[0]
    gram = total(gram)
    adjoint, grads = call(
        last_kernel,
        [((rows, owned), F32), ((3, rows, elems), F32)],
        [],
        [gram, factor0, small, basis0, basis1, values0, values1, pushed, normal, fric, slip],
    )
    return adjoint, grads


def solution(mesh):
    in_specs = (
        P(None, "brick"),
        P("brick"),
        P("brick"),
        P("brick", None),
        P("brick"),
        P("brick"),
        P("brick"),
        P("brick"),
        P("brick", None, None),
        P(),
    )
    out_specs = (P(None, "brick"), P(None, None, "brick"))
    return jax.shard_map(
        on_device, mesh=mesh, in_specs=in_specs, out_specs=out_specs, check_vma=False
    )
```

```python
import jax
import jax.numpy as jnp
from jax import lax
from jax.experimental import pallas as pl
from jax.experimental.pallas import tpu as pltpu
from jax.sharding import PartitionSpec as P

PARTS = 2
CHUNK = 16
PIVOTS = 16
VMEM_LIMIT = 48 * 1024 * 1024
AXIS = "brick"
F32 = jnp.float32
BF16 = jnp.bfloat16
NN = (((1,), (0,)), ((), ()))
NT = (((1,), (1,)), ((), ()))
TN = (((0,), (0,)), ((), ()))


def fdot(a, b, dims=NN):
    return lax.dot_general(a, b, dims, precision=lax.Precision.HIGHEST, preferred_element_type=F32)


def bdot(a, b, dims=NN):
    return lax.dot_general(a, b, dims, preferred_element_type=F32)


def lower_inverse(gram):
    n = gram.shape[0]
    row_id = lax.broadcasted_iota(jnp.int32, (n, n), 0)
    col_id = lax.broadcasted_iota(jnp.int32, (n, n), 1)
    work, side = gram, jnp.where(row_id == col_id, 1.0, 0.0).astype(F32)
    for first in range(0, n, PIVOTS):
        places = range(first, first + PIVOTS)
        cols = [jnp.broadcast_to(work[:, k : k + 1], (n, n)) for k in places]
        rows = [work[k : k + 1, :] for k in places]
        sides = [side[k : k + 1, :] for k in places]
        for j, k in enumerate(places):
            step = jnp.where(row_id > k, cols[j] * (1.0 / cols[j][k : k + 1, :]), 0.0)
            for m in range(j + 1, PIVOTS):
                at = first + m
                cols[m] = cols[m] - step * cols[j][at : at + 1, :]
                rows[m] = rows[m] - step[at : at + 1, :] * rows[j]
                sides[m] = sides[m] - step[at : at + 1, :] * sides[j]
            work = work - step * rows[j]
            side = side - step * sides[j]
    diag = jnp.sum(jnp.where(row_id == col_id, work, 0.0), axis=1, keepdims=True)
    scale = 1.0 / jnp.sqrt(diag)
    return side * scale, jnp.where(col_id >= row_id, work, 0.0) * scale


def packed(square):
    n = square.shape[0]
    fold = 128 // n
    part = n // fold
    return jnp.concatenate([square[j * part : (j + 1) * part, :] for j in range(fold)], axis=1)


def unpacked(tile):
    n = int((tile.shape[0] * 128) ** 0.5)
    fold = 128 // n
    return jnp.concatenate([tile[:, j * n : (j + 1) * n] for j in range(fold)], axis=0)


def packed_symmetric(square):
    n = square.shape[0]
    half = n // 2
    first, second, cross = square[:half, :half], square[half:, half:], square[half:, :half]
    row_id = lax.broadcasted_iota(jnp.int32, (half, half), 0)
    col_id = lax.broadcasted_iota(jnp.int32, (half, half), 1)
    both = jnp.concatenate([jnp.where(row_id >= col_id, first, second), cross], axis=1)
    fold = 128 // n
    part = half // fold
    diag = jnp.sum(jnp.where(row_id == col_id, second, 0.0), axis=0, keepdims=True)
    return jnp.concatenate(
        [
            jnp.concatenate([both[j * part : (j + 1) * part, :] for j in range(fold)], axis=1),
            jnp.concatenate([diag, jnp.zeros((1, 128 - half), F32)], axis=1),
        ],
        axis=0,
    )


def unpacked_symmetric(tile, n):
    half = n // 2
    fold = 128 // n
    part = half // fold
    both = jnp.concatenate([tile[:part, j * n : (j + 1) * n] for j in range(fold)], axis=0)
    same = lax.broadcasted_iota(jnp.int32, (n, n), 0) == lax.broadcasted_iota(jnp.int32, (n, n), 1)
    flipped = fdot(jnp.where(same, 1.0, 0.0).astype(F32), both, NT)
    mixed, cross = both[:, :half], both[:, half:]
    row_id = lax.broadcasted_iota(jnp.int32, (half, half), 0)
    col_id = lax.broadcasted_iota(jnp.int32, (half, half), 1)
    first = jnp.where(row_id >= col_id, mixed, flipped[:half])
    second = jnp.where(row_id < col_id, mixed, flipped[:half])
    second = jnp.where(row_id == col_id, jnp.broadcast_to(tile[part : part + 1, :half], (half, half)), second)
    return jnp.concatenate(
        [
            jnp.concatenate([first, flipped[half:]], axis=1),
            jnp.concatenate([cross, second], axis=1),
        ],
        axis=0,
    )


def tall(row, count):
    return jnp.broadcast_to(row, (count, row.shape[1])).astype(BF16)


def one_hot(lo_rows, depth):
    slots = lo_rows.shape[1]
    place = lax.broadcasted_iota(jnp.int32, (depth, slots), 0).astype(F32).astype(BF16)
    one, zero = jnp.ones((), BF16), jnp.zeros((), BF16)
    return jnp.concatenate(
        [
            jnp.where(place == tall(lo_rows[e : e + 1, :], depth), one, zero)
            for e in range(lo_rows.shape[0])
        ],
        axis=1,
    )


def apply_elements(
    half, conn_ref, owner_ref, coeff_ref, stacked_ref, values_ref, tiles_ref, total_ref,
    state=None, state_ref=None,
):
    rows, width = half.shape
    depth = owner_ref.shape[1]
    count = width // depth
    elems, slots = conn_ref.shape
    owner = owner_ref[...]
    below, above = one_hot(owner[0:1, :], depth), one_hot(owner[1:2, :], depth)
    tiles_ref[:rows, :] = bdot(half[:, :depth], below).astype(BF16)
    for h in range(1, count - 1):
        tiles_ref[h * rows : (h + 1) * rows, :] = half[:, h * depth : (h + 1) * depth]
    tiles_ref[(count - 1) * rows : count * rows, :] = bdot(half[:, width - depth :], above).astype(BF16)
    if state is not None:
        extra = tiles_ref.shape[0] - count * rows
        pieces = [state[:, h * depth : (h + 1) * depth] for h in range(count)]
        pieces[0] = bdot(tall(pieces[0], 16), below)[0:1, :]
        pieces[-1] = bdot(tall(pieces[-1], 16), above)[0:1, :]
        pieces.append(jnp.zeros((extra - count, depth), F32))
        tiles_ref[count * rows :, :] = jnp.concatenate(pieces, axis=0).astype(BF16)
    total_ref[...] = jnp.zeros_like(total_ref)
    zero = jnp.zeros((), BF16)

    def chunk(step, carry):
        start = pl.multiple_of(step * CHUNK, CHUNK)
        conn = conn_ref[pl.ds(start, CHUNK), :]
        hi = lax.div(conn, depth)
        hot = one_hot((conn - hi * depth).astype(F32), depth)
        spread = bdot(tiles_ref[...], hot)
        hi_wide = [tall(hi[e : e + 1, :].astype(F32), rows) for e in range(CHUNK)]
        scaled = []
        for e in range(CHUNK):
            here = slice(e * slots, (e + 1) * slots)
            value = spread[:rows, here]
            for h in range(1, count):
                value = jnp.where(
                    hi[e : e + 1, :] == h, spread[h * rows : (h + 1) * rows, here], value
                )
            values_ref[pl.ds(pl.multiple_of((start + e) * rows, rows), rows), :] = value.astype(BF16)
            scaled.append(
                jnp.concatenate(
                    [(value * coeff_ref[k, start + e]).astype(BF16) for k in range(3)], axis=1
                )
            )
            if state is not None:
                picked = spread[count * rows :, here]
                match = lax.broadcasted_iota(jnp.int32, picked.shape, 0) == hi[e : e + 1, :]
                state_ref[pl.ds(start + e, 1), :] = jnp.sum(
                    jnp.where(match, picked, 0.0), axis=0, keepdims=True
                )
        result = bdot(jnp.concatenate(scaled, axis=0), stacked_ref[...]).astype(BF16)
        masked = jnp.concatenate(
            [
                jnp.concatenate(
                    [
                        jnp.where(
                            hi_wide[e] == jnp.full((), h, BF16),
                            result[e * rows : (e + 1) * rows, :],
                            zero,
                        )
                        for e in range(CHUNK)
                    ],
                    axis=1,
                )
                for h in range(count)
            ],
            axis=0,
        )
        total_ref[...] += bdot(masked, hot, NT)
        return carry

    lax.fori_loop(0, elems // CHUNK, chunk, 0, unroll=True)
    parts = [total_ref[h * rows : (h + 1) * rows, :] for h in range(count)]
    for at, match in ((0, below), (count - 1, above)):
        top = parts[at].astype(BF16)
        rest = (parts[at] - top.astype(F32)).astype(BF16)
        both = bdot(jnp.concatenate([top, rest], axis=0), match, NT)
        parts[at] = both[:rows] + both[rows:]
    return parts


def send_bands(low, high, a_ref, b_ref):
    odd = lax.axis_index(AXIS) % 2 == 1
    a_ref[...] = jnp.where(odd, low, high)
    b_ref[...] = jnp.where(odd, high, low)


def received_bands(a_ref, b_ref):
    odd = lax.axis_index(AXIS) % 2 == 1
    a, b = a_ref[...], b_ref[...]
    return jnp.where(odd, a, b), jnp.where(odd, b, a)


def write_image(basis, parts, diag_ref, image_ref, a_ref, b_ref, state=None):
    rows, width = basis.shape
    depth = parts[0].shape[1]
    me = lax.axis_index(AXIS)
    low = parts[0] * jnp.where(me == 0, 0.0, 1.0)
    high = parts[-1] * jnp.where(me == lax.axis_size(AXIS) - 1, 0.0, 1.0)
    own = [
        diag_ref[:, (h - 1) * depth : h * depth] * basis[:, h * depth : (h + 1) * depth] + parts[h]
        for h in range(1, len(parts) - 1)
    ]
    image_ref[...] = jnp.concatenate([low] + own + [high], axis=1)
    bands = [jnp.concatenate([own[0], low], axis=1), jnp.concatenate([own[-1], high], axis=1)]
    if state is not None:
        spare = jnp.zeros((a_ref.shape[0] - rows - 1, 2 * depth), F32)
        bands = [
            jnp.concatenate([band, row, spare], axis=0)
            for band, row in zip(bands, (state[:, : 2 * depth], state[:, -2 * depth :]))
        ]
    send_bands(*bands, a_ref, b_ref)


def complete(image_ref, low, high):
    rows, width = image_ref.shape
    depth = low.shape[1] // 2
    low, high = low[:rows], high[:rows]
    return jnp.concatenate(
        [
            image_ref[:, : 2 * depth] + low,
            image_ref[:, 2 * depth : width - 2 * depth],
            image_ref[:, width - 2 * depth :] + jnp.concatenate([high[:, depth:], high[:, :depth]], axis=1),
        ],
        axis=1,
    )


def begin_kernel(sens_ref, gram_ref, a_ref, b_ref):
    sens = sens_ref[...]
    depth = a_ref.shape[1]
    owned = sens.shape[1]
    gram = packed(fdot(sens, sens, NT))
    gram_ref[...] = jnp.broadcast_to(gram[None], gram_ref.shape)
    send_bands(sens[:, :depth], sens[:, owned - depth :], a_ref, b_ref)


def first_kernel(
    gram_ref, sens_ref, disp_ref, a_in, b_in, diag_ref, conn_ref, owner_ref, coeff_ref,
    stacked_ref,
    basis_ref, image_ref, a_ref, b_ref, factor_ref, values_ref, tiles_ref, total_ref,
):
    inverse, factor = lower_inverse(unpacked(jnp.sum(gram_ref[...], axis=0)))
    factor_ref[...] = factor
    low, high = received_bands(a_in, b_in)
    basis = fdot(inverse, jnp.concatenate([low, sens_ref[...], high], axis=1))
    basis_ref[...] = basis
    parts = apply_elements(
        basis.astype(BF16), conn_ref, owner_ref, coeff_ref,
        stacked_ref, values_ref, tiles_ref, total_ref,
    )
    write_image(basis, parts, diag_ref, image_ref, a_ref, b_ref, disp_ref[...])


def own_part(field, depth):
    return field[:, depth : field.shape[1] - depth]


def middle_kernel(basis_ref, image_ref, disp_ref, a_in, b_in, full_ref, state_ref, gram_ref):
    depth = a_in.shape[1] // 2
    low, high = received_bands(a_in, b_in)
    full = complete(image_ref, low, high)
    at = full.shape[0]
    state_ref[...] = jnp.concatenate(
        [low[at : at + 1, depth:], disp_ref[...], high[at : at + 1, :depth]], axis=1
    )
    full_ref[...] = full
    own = own_part(full, depth)
    rows = own.shape[0]
    both = fdot(jnp.concatenate([own_part(basis_ref[...], depth), own], axis=0), own, NT)
    tile = jnp.concatenate([packed(both[:rows]), packed_symmetric(both[rows:])], axis=0)
    copies = gram_ref.shape[0]
    for r in range(tile.shape[0]):
        gram_ref[:, r] = jnp.broadcast_to(tile[r : r + 1, :][None], (copies, 1, 128))


def second_kernel(
    gram_ref, basis0_ref, full_ref, row_ref, diag_ref, conn_ref, owner_ref, coeff_ref,
    stacked_ref,
    basis_ref, image_ref, a_ref, b_ref, small_ref, values_ref, moved_ref,
    tiles_ref, total_ref, state_ref,
):
    summed = jnp.sum(gram_ref[...], axis=0)
    tile = jnp.concatenate([summed[r] for r in range(summed.shape[0])], axis=0)
    n = basis0_ref.shape[0]
    part = n * n // 128
    proj, square = unpacked(tile[:part]), unpacked_symmetric(tile[part:], n)
    inverse, factor = lower_inverse(square - fdot(proj, proj, TN))
    reduced = full_ref[...] - fdot(proj, basis0_ref[...], TN)
    basis = fdot(inverse, reduced)
    basis_ref[...] = basis
    small_ref[0] = proj
    small_ref[1] = square
    small_ref[2] = factor
    parts = apply_elements(
        basis.astype(BF16), conn_ref, owner_ref, coeff_ref,
        stacked_ref, values_ref, tiles_ref, total_ref, row_ref[...], state_ref,
    )
    write_image(basis, parts, diag_ref, image_ref, a_ref, b_ref)
    moved_ref[...] = state_ref[...].astype(BF16)


def side_kernel(small_in, factor0_ref, moved_ref, stacked_ref, small_ref, push_ref):
    elems, slots = moved_ref.shape
    proj, square, factor = small_in[0], small_in[1], small_in[2]
    head, unused = lower_inverse(square)
    small_ref[0] = head
    small_ref[1] = fdot(head, proj, NT)
    small_ref[2] = fdot(head, factor, NT)
    small_ref[3] = fdot(head, fdot(proj, factor0_ref[...], TN))
    moved = moved_ref[...]
    for k in range(3):
        pushed = bdot(stacked_ref[k * slots : (k + 1) * slots, :], moved, NT).astype(BF16)
        for part in range(PARTS):
            group = elems // PARTS
            push_ref[part, :, k * group : (k + 1) * group] = pushed[:, part * group : (part + 1) * group]


def late_kernel(basis0_ref, basis1_ref, image_ref, a_in, b_in, gram_ref):
    depth = a_in.shape[1] // 2
    own = own_part(complete(image_ref, *received_bands(a_in, b_in)), depth)
    rows = own.shape[0]
    every = fdot(
        jnp.concatenate(
            [own_part(basis0_ref[...], depth), own_part(basis1_ref[...], depth), own], axis=0
        ),
        own,
        NT,
    )
    gram_ref[...] = jnp.concatenate(
        [packed(every[j * rows : (j + 1) * rows]) for j in range(3)], axis=0
    )


def split3(value):
    first = value.astype(BF16)
    rest = value - first.astype(F32)
    second = rest.astype(BF16)
    return jnp.concatenate([first, second, (rest - second.astype(F32)).astype(BF16)], axis=0)


def last_kernel(
    gram_ref, factor0_ref, small_ref, basis0_ref, basis1_ref, values0_ref, values1_ref, push_ref,
    normal_ref, friction_ref, slip_ref, adjoint_ref, grads_ref,
):
    rows, width = basis0_ref.shape
    depth = (width - adjoint_ref.shape[1]) // 2
    elems = normal_ref.shape[1]
    slots = values0_ref.shape[1]
    part = gram_ref.shape[0] // 3
    p01, p11, n11 = (unpacked(gram_ref[j * part : (j + 1) * part, :]) for j in range(3))
    upper0 = factor0_ref[...]
    head, head_side = small_ref[0], small_ref[3]
    cross = fdot(small_ref[1], p01) + fdot(small_ref[2], p11)
    tail, unused = lower_inverse(n11 - fdot(cross, cross, TN))
    tail_side = fdot(tail, fdot(p01, upper0, TN) - fdot(cross, head_side, TN))
    w1_turned = fdot(tail_side, tail, TN)
    w0_turned = fdot(head_side, head, TN) - fdot(w1_turned, fdot(head, cross, TN), NT)
    turned = jnp.concatenate([w0_turned, w1_turned], axis=1)
    adjoint_ref[...] = fdot(
        turned,
        jnp.concatenate(
            [own_part(basis0_ref[...], depth), own_part(basis1_ref[...], depth)], axis=0
        ),
    )
    weights = split3(turned)
    group = elems // PARTS
    lane = lax.broadcasted_iota(jnp.int32, (rows, 3 * group), 1) % group
    found = []
    for part in range(PARTS):
        pairs = jnp.zeros((rows, 3 * group), F32)
        for start in range(part * group, (part + 1) * group, CHUNK):
            fields = []
            for ref in (values0_ref, values1_ref):
                block = ref[start * rows : (start + CHUNK) * rows, :]
                fields.append(
                    jnp.concatenate([block[e * rows : (e + 1) * rows, :] for e in range(CHUNK)], axis=1)
                )
            mixed = bdot(weights, jnp.concatenate(fields, axis=0))
            mixed = (mixed[:rows] + (mixed[rows : 2 * rows] + mixed[2 * rows :])).astype(BF16)
            every = bdot(
                jnp.concatenate([mixed[:, e * slots : (e + 1) * slots] for e in range(CHUNK)], axis=0),
                push_ref[part],
            )
            for e in range(CHUNK):
                at = start - part * group + e
                pairs = jnp.where(lane == at, every[e * rows : (e + 1) * rows, :], pairs)
        found.append(pairs)
    pairs = [
        jnp.concatenate([part[:, k * group : (k + 1) * group] for part in found], axis=1)
        for k in range(3)
    ]
    slip = slip_ref[...].astype(F32)
    grads_ref[0] = -(pairs[0] + slip * friction_ref[...] * pairs[2])
    grads_ref[1] = -pairs[1]
    grads_ref[2] = -slip * normal_ref[...] * pairs[2]


def call(kernel, outs, scratch, args, smem=()):
    return pl.pallas_call(
        kernel,
        out_shape=[jax.ShapeDtypeStruct(shape, dtype) for shape, dtype in outs],
        in_specs=[
            pl.BlockSpec(memory_space=pltpu.SMEM if i in smem else pltpu.VMEM)
            for i in range(len(args))
        ],
        out_specs=[pl.BlockSpec(memory_space=pltpu.VMEM) for unused in outs],
        scratch_shapes=[pltpu.VMEM(shape, dtype) for shape, dtype in scratch],
        compiler_params=pltpu.CompilerParams(vmem_limit_bytes=VMEM_LIMIT),
    )(*args)


def exchanged(a, b):
    count = lax.axis_size(AXIS)
    first = [(i, i ^ 1) for i in range(count) if i ^ 1 < count]
    other = [(i, i + 1 if i % 2 else i - 1) for i in range(count)]
    second = [(i, j) for i, j in other if 0 <= j < count]
    return lax.ppermute(a, AXIS, first), lax.ppermute(b, AXIS, second)


def everyones(copies):
    return lax.all_to_all(copies, AXIS, 0, 0, tiled=True)


def total(value):
    count = lax.axis_size(AXIS)
    stride = 1
    while stride < count:
        left = count // stride
        radix = 2 if stride == 1 or left % 4 else 4
        parts = [value]
        for d in range(1, radix):
            route = []
            for i in range(count):
                digit = (i // stride) % radix
                route.append((i, i + ((digit ^ d) - digit) * stride))
            parts.append(lax.ppermute(value, AXIS, route))
        while len(parts) > 1:
            parts = [parts[2 * i] + parts[2 * i + 1] for i in range(len(parts) // 2)]
        value = parts[0]
        stride *= radix
    return value


def on_device(
    sensitivity, diagonal, displacement, connectivity, normal_stiff, shear_stiff, friction, slip_state,
    owner_map, templates,
):
    devices = lax.axis_size(AXIS)
    rows, owned = sensitivity.shape
    depth = owner_map.shape[2]
    elems, slots = connectivity.shape
    width = owned + 2 * depth
    count = width // depth
    part = rows * rows // 128
    extra = -(-count // 16) * 16
    wide = ((rows, width), F32)
    band = ((rows, 2 * depth), F32)
    picked = ((elems * rows, slots), BF16)

    line = lambda array: array[None, :]
    disp, diag = line(displacement.astype(F32)), line(diagonal)
    normal, fric, slip = line(normal_stiff), line(friction), line(slip_state)
    owner = owner_map[0].astype(F32)
    stacked = templates.reshape(3 * slots, slots)

    coeffs = jnp.stack([normal_stiff, shear_stiff, slip_state.astype(F32) * friction * normal_stiff])

    gram, a, b = call(
        begin_kernel,
        [((devices, part, 128), F32), ((rows, depth), F32), ((rows, depth), F32)],
        [],
        [sensitivity],
    )
    a, b = exchanged(a, b)
    gram = everyones(gram)
    taller = ((rows + 8, 2 * depth), F32)
    basis0, image, a, b, factor0, values0 = call(
        first_kernel,
        [wide, wide, taller, taller, ((rows, rows), F32), picked],
        [((count * rows, depth), BF16), ((count * rows, depth), F32)],
        [gram, sensitivity, disp, a, b, diag, connectivity, owner, coeffs, stacked],
        smem=(8,),
    )
    a, b = exchanged(a, b)
    full, state, gram = call(
        middle_kernel,
        [wide, ((1, width), F32), ((devices, part + part // 2 + 1, 1, 128), F32)],
        [],
        [basis0, image, disp, a, b],
    )
    gram = everyones(gram)
    basis1, image, a, b, small, values1, moved = call(
        second_kernel,
        [wide, wide, band, band, ((3, rows, rows), F32), picked, ((elems, slots), BF16)],
        [((count * rows + extra, depth), BF16), ((count * rows, depth), F32), ((elems, slots), F32)],
        [gram, basis0, full, state, diag, connectivity, owner, coeffs, stacked],
        smem=(7,),
    )
    a, b = exchanged(a, b)
    small, pushed = call(
        side_kernel,
        [((4, rows, rows), F32), ((PARTS, slots, 3 * elems // PARTS), BF16)],
        [],
        [small, factor0, moved, stacked],
    )
    image, small, pushed = lax.optimization_barrier((image, small, pushed))
    gram = call(late_kernel, [((3 * part, 128), F32)], [], [basis0, basis1, image, a, b])[0]
    gram = total(gram)
    adjoint, grads = call(
        last_kernel,
        [((rows, owned), F32), ((3, rows, elems), F32)],
        [],
        [gram, factor0, small, basis0, basis1, values0, values1, pushed, normal, fric, slip],
    )
    return adjoint, grads


def solution(mesh):
    in_specs = (
        P(None, "brick"),
        P("brick"),
        P("brick"),
        P("brick", None),
        P("brick"),
        P("brick"),
        P("brick"),
        P("brick"),
        P("brick", None, None),
        P(),
    )
    out_specs = (P(None, "brick"), P(None, None, "brick"))
    return jax.shard_map(
        on_device, mesh=mesh, in_specs=in_specs, out_specs=out_specs, check_vma=False
    )
```

```python
import jax
import jax.numpy as jnp
from jax import lax
from jax.experimental import pallas as pl
from jax.experimental.pallas import tpu as pltpu
from jax.sharding import PartitionSpec as P

PARTS = 2
CHUNK = 16
PIVOTS = 16
VMEM_LIMIT = 48 * 1024 * 1024
AXIS = "brick"
F32 = jnp.float32
BF16 = jnp.bfloat16
NN = (((1,), (0,)), ((), ()))
NT = (((1,), (1,)), ((), ()))
TN = (((0,), (0,)), ((), ()))


def fdot(a, b, dims=NN):
    return lax.dot_general(a, b, dims, precision=lax.Precision.HIGHEST, preferred_element_type=F32)


def bdot(a, b, dims=NN):
    return lax.dot_general(a, b, dims, preferred_element_type=F32)


def lower_inverse(gram):
    n = gram.shape[0]
    row_id = lax.broadcasted_iota(jnp.int32, (n, n), 0)
    col_id = lax.broadcasted_iota(jnp.int32, (n, n), 1)
    work, side = gram, jnp.where(row_id == col_id, 1.0, 0.0).astype(F32)
    for first in range(0, n, PIVOTS):
        places = range(first, first + PIVOTS)
        cols = [jnp.broadcast_to(work[:, k : k + 1], (n, n)) for k in places]
        rows = [work[k : k + 1, :] for k in places]
        sides = [side[k : k + 1, :] for k in places]
        for j, k in enumerate(places):
            step = jnp.where(row_id > k, cols[j] * (1.0 / cols[j][k : k + 1, :]), 0.0)
            for m in range(j + 1, PIVOTS):
                at = first + m
                cols[m] = cols[m] - step * cols[j][at : at + 1, :]
                rows[m] = rows[m] - step[at : at + 1, :] * rows[j]
                sides[m] = sides[m] - step[at : at + 1, :] * sides[j]
            work = work - step * rows[j]
            side = side - step * sides[j]
    diag = jnp.sum(jnp.where(row_id == col_id, work, 0.0), axis=1, keepdims=True)
    scale = 1.0 / jnp.sqrt(diag)
    return side * scale, jnp.where(col_id >= row_id, work, 0.0) * scale


def packed(square):
    n = square.shape[0]
    fold = 128 // n
    part = n // fold
    return jnp.concatenate([square[j * part : (j + 1) * part, :] for j in range(fold)], axis=1)


def unpacked(tile):
    n = int((tile.shape[0] * 128) ** 0.5)
    fold = 128 // n
    return jnp.concatenate([tile[:, j * n : (j + 1) * n] for j in range(fold)], axis=0)


def packed_symmetric(square):
    n = square.shape[0]
    half = n // 2
    first, second, cross = square[:half, :half], square[half:, half:], square[half:, :half]
    row_id = lax.broadcasted_iota(jnp.int32, (half, half), 0)
    col_id = lax.broadcasted_iota(jnp.int32, (half, half), 1)
    both = jnp.concatenate([jnp.where(row_id >= col_id, first, second), cross], axis=1)
    fold = 128 // n
    part = half // fold
    diag = jnp.sum(jnp.where(row_id == col_id, second, 0.0), axis=0, keepdims=True)
    return jnp.concatenate(
        [
            jnp.concatenate([both[j * part : (j + 1) * part, :] for j in range(fold)], axis=1),
            jnp.concatenate([diag, jnp.zeros((1, 128 - half), F32)], axis=1),
        ],
        axis=0,
    )


def unpacked_symmetric(tile, n):
    half = n // 2
    fold = 128 // n
    part = half // fold
    both = jnp.concatenate([tile[:part, j * n : (j + 1) * n] for j in range(fold)], axis=0)
    same = lax.broadcasted_iota(jnp.int32, (n, n), 0) == lax.broadcasted_iota(jnp.int32, (n, n), 1)
    flipped = fdot(jnp.where(same, 1.0, 0.0).astype(F32), both, NT)
    mixed, cross = both[:, :half], both[:, half:]
    row_id = lax.broadcasted_iota(jnp.int32, (half, half), 0)
    col_id = lax.broadcasted_iota(jnp.int32, (half, half), 1)
    first = jnp.where(row_id >= col_id, mixed, flipped[:half])
    second = jnp.where(row_id < col_id, mixed, flipped[:half])
    second = jnp.where(row_id == col_id, jnp.broadcast_to(tile[part : part + 1, :half], (half, half)), second)
    return jnp.concatenate(
        [
            jnp.concatenate([first, flipped[half:]], axis=1),
            jnp.concatenate([cross, second], axis=1),
        ],
        axis=0,
    )


def tall(row, count):
    return jnp.broadcast_to(row, (count, row.shape[1])).astype(BF16)


def one_hot(lo_rows, depth):
    slots = lo_rows.shape[1]
    place = lax.broadcasted_iota(jnp.int32, (depth, slots), 0).astype(F32).astype(BF16)
    one, zero = jnp.ones((), BF16), jnp.zeros((), BF16)
    return jnp.concatenate(
        [
            jnp.where(place == tall(lo_rows[e : e + 1, :], depth), one, zero)
            for e in range(lo_rows.shape[0])
        ],
        axis=1,
    )


def apply_elements(
    half, conn_ref, owner_ref, coeff_ref, stacked_ref, values_ref, tiles_ref, total_ref,
    state=None, state_ref=None,
):
    rows, width = half.shape
    depth = owner_ref.shape[1]
    count = width // depth
    elems, slots = conn_ref.shape
    owner = owner_ref[...]
    below, above = one_hot(owner[0:1, :], depth), one_hot(owner[1:2, :], depth)
    tiles_ref[:rows, :] = bdot(half[:, :depth], below).astype(BF16)
    for h in range(1, count - 1):
        tiles_ref[h * rows : (h + 1) * rows, :] = half[:, h * depth : (h + 1) * depth]
    tiles_ref[(count - 1) * rows : count * rows, :] = bdot(half[:, width - depth :], above).astype(BF16)
    if state is not None:
        extra = tiles_ref.shape[0] - count * rows
        pieces = [state[:, h * depth : (h + 1) * depth] for h in range(count)]
        pieces[0] = bdot(tall(pieces[0], 16), below)[0:1, :]
        pieces[-1] = bdot(tall(pieces[-1], 16), above)[0:1, :]
        pieces.append(jnp.zeros((extra - count, depth), F32))
        tiles_ref[count * rows :, :] = jnp.concatenate(pieces, axis=0).astype(BF16)
    total_ref[...] = jnp.zeros_like(total_ref)
    zero = jnp.zeros((), BF16)

    def chunk(step, carry):
        start = pl.multiple_of(step * CHUNK, CHUNK)
        conn = conn_ref[pl.ds(start, CHUNK), :]
        hi = lax.div(conn, depth)
        hot = one_hot((conn - hi * depth).astype(F32), depth)
        spread = bdot(tiles_ref[...], hot)
        hi_wide = [tall(hi[e : e + 1, :].astype(F32), rows) for e in range(CHUNK)]
        scaled = []
        for e in range(CHUNK):
            here = slice(e * slots, (e + 1) * slots)
            value = spread[:rows, here]
            for h in range(1, count):
                value = jnp.where(
                    hi[e : e + 1, :] == h, spread[h * rows : (h + 1) * rows, here], value
                )
            values_ref[pl.ds(pl.multiple_of((start + e) * rows, rows), rows), :] = value.astype(BF16)
            scaled.append(
                jnp.concatenate(
                    [(value * coeff_ref[k, start + e]).astype(BF16) for k in range(3)], axis=1
                )
            )
            if state is not None:
                picked = spread[count * rows :, here]
                match = lax.broadcasted_iota(jnp.int32, picked.shape, 0) == hi[e : e + 1, :]
                state_ref[pl.ds(start + e, 1), :] = jnp.sum(
                    jnp.where(match, picked, 0.0), axis=0, keepdims=True
                )
        result = bdot(jnp.concatenate(scaled, axis=0), stacked_ref[...]).astype(BF16)
        masked = jnp.concatenate(
            [
                jnp.concatenate(
                    [
                        jnp.where(
                            hi_wide[e] == jnp.full((), h, BF16),
                            result[e * rows : (e + 1) * rows, :],
                            zero,
                        )
                        for e in range(CHUNK)
                    ],
                    axis=1,
                )
                for h in range(count)
            ],
            axis=0,
        )
        total_ref[...] += bdot(masked, hot, NT)
        return carry

    lax.fori_loop(0, elems // CHUNK, chunk, 0, unroll=True)
    parts = [total_ref[h * rows : (h + 1) * rows, :] for h in range(count)]
    for at, match in ((0, below), (count - 1, above)):
        top = parts[at].astype(BF16)
        rest = (parts[at] - top.astype(F32)).astype(BF16)
        both = bdot(jnp.concatenate([top, rest], axis=0), match, NT)
        parts[at] = both[:rows] + both[rows:]
    return parts


def send_bands(low, high, a_ref, b_ref):
    odd = lax.axis_index(AXIS) % 2 == 1
    a_ref[...] = jnp.where(odd, low, high)
    b_ref[...] = jnp.where(odd, high, low)


def received_bands(a_ref, b_ref):
    odd = lax.axis_index(AXIS) % 2 == 1
    a, b = a_ref[...], b_ref[...]
    return jnp.where(odd, a, b), jnp.where(odd, b, a)


def write_image(basis, parts, diag_ref, image_ref, a_ref, b_ref, state=None):
    rows, width = basis.shape
    depth = parts[0].shape[1]
    me = lax.axis_index(AXIS)
    low = parts[0] * jnp.where(me == 0, 0.0, 1.0)
    high = parts[-1] * jnp.where(me == lax.axis_size(AXIS) - 1, 0.0, 1.0)
    own = [
        diag_ref[:, (h - 1) * depth : h * depth] * basis[:, h * depth : (h + 1) * depth] + parts[h]
        for h in range(1, len(parts) - 1)
    ]
    image_ref[...] = jnp.concatenate([low] + own + [high], axis=1)
    bands = [jnp.concatenate([own[0], low], axis=1), jnp.concatenate([own[-1], high], axis=1)]
    if state is not None:
        spare = jnp.zeros((a_ref.shape[0] - rows - 1, 2 * depth), F32)
        bands = [
            jnp.concatenate([band, row, spare], axis=0)
            for band, row in zip(bands, (state[:, : 2 * depth], state[:, -2 * depth :]))
        ]
    send_bands(*bands, a_ref, b_ref)


def complete(image_ref, low, high):
    rows, width = image_ref.shape
    depth = low.shape[1] // 2
    low, high = low[:rows], high[:rows]
    return jnp.concatenate(
        [
            image_ref[:, : 2 * depth] + low,
            image_ref[:, 2 * depth : width - 2 * depth],
            image_ref[:, width - 2 * depth :] + jnp.concatenate([high[:, depth:], high[:, :depth]], axis=1),
        ],
        axis=1,
    )


def begin_kernel(sens_ref, gram_ref, a_ref, b_ref):
    sens = sens_ref[...]
    depth = a_ref.shape[1]
    owned = sens.shape[1]
    gram = packed(fdot(sens, sens, NT))
    gram_ref[...] = jnp.broadcast_to(gram[None], gram_ref.shape)
    send_bands(sens[:, :depth], sens[:, owned - depth :], a_ref, b_ref)


def first_kernel(
    gram_ref, sens_ref, disp_ref, a_in, b_in, diag_ref, conn_ref, owner_ref, coeff_ref,
    stacked_ref,
    basis_ref, image_ref, a_ref, b_ref, factor_ref, values_ref, tiles_ref, total_ref,
):
    inverse, factor = lower_inverse(unpacked(jnp.sum(gram_ref[...], axis=0)))
    factor_ref[...] = factor
    low, high = received_bands(a_in, b_in)
    basis = fdot(inverse, jnp.concatenate([low, sens_ref[...], high], axis=1))
    basis_ref[...] = basis
    parts = apply_elements(
        basis.astype(BF16), conn_ref, owner_ref, coeff_ref,
        stacked_ref, values_ref, tiles_ref, total_ref,
    )
    write_image(basis, parts, diag_ref, image_ref, a_ref, b_ref, disp_ref[...])


def own_part(field, depth):
    return field[:, depth : field.shape[1] - depth]


def edge_part(field, depth):
    width = field.shape[1]
    return jnp.concatenate([field[:, depth : 2 * depth], field[:, width - 2 * depth : width - depth]], axis=1)


def inner_kernel(owner_ref, *refs):
    *field_refs, out_ref = refs
    depth = owner_ref.shape[1]
    fields = [own_part(ref[...], 2 * depth) for ref in field_refs]
    out_ref[...] = fdot(jnp.concatenate(fields, axis=0), fields[-1], NT)


def middle_kernel(basis_ref, image_ref, inner_ref, disp_ref, a_in, b_in, full_ref, state_ref, gram_ref):
    depth = a_in.shape[1] // 2
    low, high = received_bands(a_in, b_in)
    full = complete(image_ref, low, high)
    at = full.shape[0]
    state_ref[...] = jnp.concatenate(
        [low[at : at + 1, depth:], disp_ref[...], high[at : at + 1, :depth]], axis=1
    )
    full_ref[...] = full
    edge = edge_part(full, depth)
    rows = edge.shape[0]
    both = inner_ref[...] + fdot(
        jnp.concatenate([edge_part(basis_ref[...], depth), edge], axis=0), edge, NT
    )
    tile = jnp.concatenate([packed(both[:rows]), packed_symmetric(both[rows:])], axis=0)
    copies = gram_ref.shape[0]
    for r in range(tile.shape[0]):
        gram_ref[:, r] = jnp.broadcast_to(tile[r : r + 1, :][None], (copies, 1, 128))


def second_kernel(
    gram_ref, basis0_ref, full_ref, row_ref, diag_ref, conn_ref, owner_ref, coeff_ref,
    stacked_ref,
    basis_ref, image_ref, a_ref, b_ref, small_ref, values_ref, moved_ref,
    tiles_ref, total_ref, state_ref,
):
    summed = jnp.sum(gram_ref[...], axis=0)
    tile = jnp.concatenate([summed[r] for r in range(summed.shape[0])], axis=0)
    n = basis0_ref.shape[0]
    part = n * n // 128
    proj, square = unpacked(tile[:part]), unpacked_symmetric(tile[part:], n)
    inverse, factor = lower_inverse(square - fdot(proj, proj, TN))
    reduced = full_ref[...] - fdot(proj, basis0_ref[...], TN)
    basis = fdot(inverse, reduced)
    basis_ref[...] = basis
    small_ref[0] = proj
    small_ref[1] = square
    small_ref[2] = factor
    parts = apply_elements(
        basis.astype(BF16), conn_ref, owner_ref, coeff_ref,
        stacked_ref, values_ref, tiles_ref, total_ref, row_ref[...], state_ref,
    )
    write_image(basis, parts, diag_ref, image_ref, a_ref, b_ref)
    moved_ref[...] = state_ref[...].astype(BF16)


def side_kernel(small_in, factor0_ref, moved_ref, stacked_ref, small_ref, push_ref):
    elems, slots = moved_ref.shape
    proj, square, factor = small_in[0], small_in[1], small_in[2]
    head, unused = lower_inverse(square)
    small_ref[0] = head
    small_ref[1] = fdot(head, proj, NT)
    small_ref[2] = fdot(head, factor, NT)
    small_ref[3] = fdot(head, fdot(proj, factor0_ref[...], TN))
    moved = moved_ref[...]
    for k in range(3):
        pushed = bdot(stacked_ref[k * slots : (k + 1) * slots, :], moved, NT).astype(BF16)
        for part in range(PARTS):
            group = elems // PARTS
            push_ref[part, :, k * group : (k + 1) * group] = pushed[:, part * group : (part + 1) * group]


def late_kernel(basis0_ref, basis1_ref, image_ref, inner_ref, a_in, b_in, gram_ref):
    depth = a_in.shape[1] // 2
    edge = edge_part(complete(image_ref, *received_bands(a_in, b_in)), depth)
    rows = edge.shape[0]
    every = inner_ref[...] + fdot(
        jnp.concatenate(
            [edge_part(basis0_ref[...], depth), edge_part(basis1_ref[...], depth), edge], axis=0
        ),
        edge,
        NT,
    )
    gram_ref[...] = jnp.concatenate(
        [packed(every[j * rows : (j + 1) * rows]) for j in range(3)], axis=0
    )


def split3(value):
    first = value.astype(BF16)
    rest = value - first.astype(F32)
    second = rest.astype(BF16)
    return jnp.concatenate([first, second, (rest - second.astype(F32)).astype(BF16)], axis=0)


def last_kernel(
    gram_ref, factor0_ref, small_ref, basis0_ref, basis1_ref, values0_ref, values1_ref, push_ref,
    normal_ref, friction_ref, slip_ref, adjoint_ref, grads_ref,
):
    rows, width = basis0_ref.shape
    depth = (width - adjoint_ref.shape[1]) // 2
    elems = normal_ref.shape[1]
    slots = values0_ref.shape[1]
    part = gram_ref.shape[0] // 3
    p01, p11, n11 = (unpacked(gram_ref[j * part : (j + 1) * part, :]) for j in range(3))
    upper0 = factor0_ref[...]
    head, head_side = small_ref[0], small_ref[3]
    cross = fdot(small_ref[1], p01) + fdot(small_ref[2], p11)
    tail, unused = lower_inverse(n11 - fdot(cross, cross, TN))
    tail_side = fdot(tail, fdot(p01, upper0, TN) - fdot(cross, head_side, TN))
    w1_turned = fdot(tail_side, tail, TN)
    w0_turned = fdot(head_side, head, TN) - fdot(w1_turned, fdot(head, cross, TN), NT)
    turned = jnp.concatenate([w0_turned, w1_turned], axis=1)
    adjoint_ref[...] = fdot(
        turned,
        jnp.concatenate(
            [own_part(basis0_ref[...], depth), own_part(basis1_ref[...], depth)], axis=0
        ),
    )
    weights = split3(turned)
    group = elems // PARTS
    lane = lax.broadcasted_iota(jnp.int32, (rows, 3 * group), 1) % group
    found = []
    for part in range(PARTS):
        pairs = jnp.zeros((rows, 3 * group), F32)
        for start in range(part * group, (part + 1) * group, CHUNK):
            fields = []
            for ref in (values0_ref, values1_ref):
                block = ref[start * rows : (start + CHUNK) * rows, :]
                fields.append(
                    jnp.concatenate([block[e * rows : (e + 1) * rows, :] for e in range(CHUNK)], axis=1)
                )
            mixed = bdot(weights, jnp.concatenate(fields, axis=0))
            mixed = (mixed[:rows] + (mixed[rows : 2 * rows] + mixed[2 * rows :])).astype(BF16)
            every = bdot(
                jnp.concatenate([mixed[:, e * slots : (e + 1) * slots] for e in range(CHUNK)], axis=0),
                push_ref[part],
            )
            for e in range(CHUNK):
                at = start - part * group + e
                pairs = jnp.where(lane == at, every[e * rows : (e + 1) * rows, :], pairs)
        found.append(pairs)
    pairs = [
        jnp.concatenate([part[:, k * group : (k + 1) * group] for part in found], axis=1)
        for k in range(3)
    ]
    slip = slip_ref[...].astype(F32)
    grads_ref[0] = -(pairs[0] + slip * friction_ref[...] * pairs[2])
    grads_ref[1] = -pairs[1]
    grads_ref[2] = -slip * normal_ref[...] * pairs[2]


def call(kernel, outs, scratch, args, smem=()):
    return pl.pallas_call(
        kernel,
        out_shape=[jax.ShapeDtypeStruct(shape, dtype) for shape, dtype in outs],
        in_specs=[
            pl.BlockSpec(memory_space=pltpu.SMEM if i in smem else pltpu.VMEM)
            for i in range(len(args))
        ],
        out_specs=[pl.BlockSpec(memory_space=pltpu.VMEM) for unused in outs],
        scratch_shapes=[pltpu.VMEM(shape, dtype) for shape, dtype in scratch],
        compiler_params=pltpu.CompilerParams(vmem_limit_bytes=VMEM_LIMIT),
    )(*args)


def exchanged(a, b):
    count = lax.axis_size(AXIS)
    first = [(i, i ^ 1) for i in range(count) if i ^ 1 < count]
    other = [(i, i + 1 if i % 2 else i - 1) for i in range(count)]
    second = [(i, j) for i, j in other if 0 <= j < count]
    return lax.ppermute(a, AXIS, first), lax.ppermute(b, AXIS, second)


def everyones(copies):
    return lax.all_to_all(copies, AXIS, 0, 0, tiled=True)


def total(value):
    count = lax.axis_size(AXIS)
    stride = 1
    while stride < count:
        left = count // stride
        radix = 2 if stride == 1 or left % 4 else 4
        parts = [value]
        for d in range(1, radix):
            route = []
            for i in range(count):
                digit = (i // stride) % radix
                route.append((i, i + ((digit ^ d) - digit) * stride))
            parts.append(lax.ppermute(value, AXIS, route))
        while len(parts) > 1:
            parts = [parts[2 * i] + parts[2 * i + 1] for i in range(len(parts) // 2)]
        value = parts[0]
        stride *= radix
    return value


def on_device(
    sensitivity, diagonal, displacement, connectivity, normal_stiff, shear_stiff, friction, slip_state,
    owner_map, templates,
):
    devices = lax.axis_size(AXIS)
    rows, owned = sensitivity.shape
    depth = owner_map.shape[2]
    elems, slots = connectivity.shape
    width = owned + 2 * depth
    count = width // depth
    part = rows * rows // 128
    extra = -(-count // 16) * 16
    wide = ((rows, width), F32)
    band = ((rows, 2 * depth), F32)
    picked = ((elems * rows, slots), BF16)

    line = lambda array: array[None, :]
    disp, diag = line(displacement.astype(F32)), line(diagonal)
    normal, fric, slip = line(normal_stiff), line(friction), line(slip_state)
    owner = owner_map[0].astype(F32)
    stacked = templates.reshape(3 * slots, slots)

    coeffs = jnp.stack([normal_stiff, shear_stiff, slip_state.astype(F32) * friction * normal_stiff])

    gram, a, b = call(
        begin_kernel,
        [((devices, part, 128), F32), ((rows, depth), F32), ((rows, depth), F32)],
        [],
        [sensitivity],
    )
    a, b = exchanged(a, b)
    gram = everyones(gram)
    taller = ((rows + 8, 2 * depth), F32)
    basis0, image, a, b, factor0, values0 = call(
        first_kernel,
        [wide, wide, taller, taller, ((rows, rows), F32), picked],
        [((count * rows, depth), BF16), ((count * rows, depth), F32)],
        [gram, sensitivity, disp, a, b, diag, connectivity, owner, coeffs, stacked],
        smem=(8,),
    )
    a, b = exchanged(a, b)
    inner = call(inner_kernel, [((2 * rows, rows), F32)], [], [owner, basis0, image])[0]
    full, state, gram = call(
        middle_kernel,
        [wide, ((1, width), F32), ((devices, part + part // 2 + 1, 1, 128), F32)],
        [],
        [basis0, image, inner, disp, a, b],
    )
    gram = everyones(gram)
    basis1, image, a, b, small, values1, moved = call(
        second_kernel,
        [wide, wide, band, band, ((3, rows, rows), F32), picked, ((elems, slots), BF16)],
        [((count * rows + extra, depth), BF16), ((count * rows, depth), F32), ((elems, slots), F32)],
        [gram, basis0, full, state, diag, connectivity, owner, coeffs, stacked],
        smem=(7,),
    )
    a, b = exchanged(a, b)
    small, pushed = call(
        side_kernel,
        [((4, rows, rows), F32), ((PARTS, slots, 3 * elems // PARTS), BF16)],
        [],
        [small, factor0, moved, stacked],
    )
    inner = call(inner_kernel, [((3 * rows, rows), F32)], [], [owner, basis0, basis1, image])[0]
    image, small, pushed = lax.optimization_barrier((image, small, pushed))
    gram = call(late_kernel, [((3 * part, 128), F32)], [], [basis0, basis1, image, inner, a, b])[0]
    gram = total(gram)
    adjoint, grads = call(
        last_kernel,
        [((rows, owned), F32), ((3, rows, elems), F32)],
        [],
        [gram, factor0, small, basis0, basis1, values0, values1, pushed, normal, fric, slip],
    )
    return adjoint, grads


def solution(mesh):
    in_specs = (
        P(None, "brick"),
        P("brick"),
        P("brick"),
        P("brick", None),
        P("brick"),
        P("brick"),
        P("brick"),
        P("brick"),
        P("brick", None, None),
        P(),
    )
    out_specs = (P(None, "brick"), P(None, None, "brick"))
    return jax.shard_map(
        on_device, mesh=mesh, in_specs=in_specs, out_specs=out_specs, check_vma=False
    )
```
